256 devices in a mesh: row: 16 (over z, x_hi), col: 16 (over y, x_lo, core).
Axes of the slice: x: 4 (x_hi: 2, x_lo: 2; x = x_hi * 2 + x_lo), y: 4, z: 8, core: 2. Of those that a mesh axis runs over, the one named last changes fastest.
Arguments:
- query_rows: bfloat16 [128, 256, 2048], P('row', 'col'), may hold values from -6 to 6
- key_rows: bfloat16 [128, 256, 2048], P('row', 'col'), may hold values from -6 to 6
- value_rows: bfloat16 [128, 256, 2048], P('row', 'col'), may hold values from -6 to 6
- grad_out: bfloat16 [128, 256, 2048], P('row', 'col'), may hold values from -48 to 48
- log_norm: float32 [128, 256, 16], P('row', 'col'), may hold values from 5.5 to 7.5
- grad_offset: float32 [128, 256, 16], P('row', 'col'), may hold values from -192 to 192
- listed: int32 [256, 64], P(('row', 'col')), may hold values from 0 to 255, all different within a row
Outputs:
- grad_query: float32 [128, 256, 2048], P('row', 'col')
- grad_key: float32 [128, 256, 2048], P('row', 'col')
- grad_value: float32 [128, 256, 2048], P('row', 'col')
The draws below stay inside these ranges and needn't reach their ends.
Inputs may be any that keep to these rules, and one draw needn't show every extreme that they name: Each query block lists 64 different summary blocks; every block is listed by some query block.
All inputs are finite; a program needn't handle non-finite values.
Results may differ from the reference program's by a relative error of at most 0.0034.
Values may be sent and summed in bfloat16 or wider, within the bound.
A program may use at most 128 MiB of HBM per device.

```python
import math
import jax
import jax.numpy as jnp
from jax import lax

D_HEAD = 128
HEADS = 16
TR = 8
TC = 16
D = 2048
NB = 256
SEL = 64
IMG_R = 128
IMG_C = 256
N_ROW = 16
N_COL = 16


def shard_levels(stream_key, shape, cuts, low, high):
    level, own = 1.0, jax.random.fold_in(stream_key, 6)
    for position, shards_of in cuts:
        steps = jnp.exp(jax.random.uniform(jax.random.fold_in(own, position), (shards_of,), jnp.float32, low / len(cuts), high / len(cuts)))
        level = level * jnp.repeat(steps, shape[position] // shards_of).reshape([-1 if axis == position else 1 for axis in range(len(shape))])
    return level


def picks_of(rng, rows, count, top, lift):
    order = jax.random.permutation(jax.random.fold_in(rng, 1), count)
    favour = order
    for power in range(3):
        favour = favour * favour // count
    favour = favour * lift // count
    chance = jax.random.randint(jax.random.fold_in(rng, 2), (rows, count), 0, 4096) + favour
    fixed_rows = jax.random.permutation(jax.random.fold_in(rng, 3), rows)[jnp.arange(count) % rows]
    chance = jnp.where(jnp.arange(rows)[:, None] == fixed_rows[None, :], 1 << 14, chance)
    priority = chance * count + jnp.arange(count)
    return lax.top_k(priority.astype(jnp.int32), top)[1].astype(jnp.int32)


def centred(rng, dims, width, limit, shards=(), held_as=jnp.bfloat16):
    level = shard_levels(rng, dims, shards, -0.22, 0.18) if shards else 1.0
    values = jax.random.normal(rng, dims, jnp.float32) * width * level
    return jnp.minimum(jnp.maximum(values, -limit), limit).astype(held_as)


def setup_inputs(seed: int = 0) -> dict:
    keys = jax.random.split(jax.random.key(seed), 8)
    return {
        "query_rows": centred(keys[0], (IMG_R, IMG_C, D), 1.0, 6.0, ((0, 16), (1, 16))),
        "key_rows": centred(keys[1], (IMG_R, IMG_C, D), 1.0, 6.0, ((0, 16), (1, 16))),
        "value_rows": centred(keys[2], (IMG_R, IMG_C, D), 1.0, 6.0, ((0, 16), (1, 16))),
        "grad_out": centred(keys[3], (IMG_R, IMG_C, D), 8.0, 48.0, ((0, 16), (1, 16))),
        "log_norm": jnp.clip(5.5 + 2.0 * jax.random.uniform(keys[4], (IMG_R, IMG_C, HEADS), jnp.float32) ** shard_levels(keys[4], (IMG_R, IMG_C, HEADS), ((0, 16), (1, 16)), -0.2, 0.2), 5.5, 7.5),
        "grad_offset": centred(keys[5], (IMG_R, IMG_C, HEADS), 32.0, 192.0, ((0, 16), (1, 16)), jnp.float32),
        "listed": picks_of(keys[6], NB, NB, SEL, 0),
    }


def grid_coords(first_row, first_column, count_rows, count_columns):
    row_index = first_row + jnp.arange(count_rows, dtype=jnp.int32)
    column_index = first_column + jnp.arange(count_columns, dtype=jnp.int32)
    return (jnp.broadcast_to(row_index[:, None], (count_rows, count_columns)).reshape(-1), jnp.broadcast_to(column_index[None, :], (count_rows, count_columns)).reshape(-1))

def window_mask(query_at, target_at, radius, limits):
    nearby = (jnp.abs(query_at[0][:, None] - target_at[0][None, :]) <= radius) & (jnp.abs(query_at[1][:, None] - target_at[1][None, :]) <= radius)
    query_inside = (query_at[0] >= 0) & (query_at[0] < limits[0]) & (query_at[1] >= 0) & (query_at[1] < limits[1])
    target_inside = (target_at[0] >= 0) & (target_at[0] < limits[0]) & (target_at[1] >= 0) & (target_at[1] < limits[1])
    return nearby & query_inside[:, None] & target_inside[None, :]

def group_grads(query_part, grad_part, norm_part, offset_part, key_part, value_part, allowed, wanted):
    query_count = query_part.shape[0]
    key_count = key_part.shape[0]
    group_heads = norm_part.shape[1]
    head_size = query_part.shape[1] // group_heads
    score_scale = 1.0 / math.sqrt(head_size)
    query_three = query_part.reshape(query_count, group_heads, head_size).astype(jnp.float32)
    grad_three = grad_part.reshape(query_count, group_heads, head_size).astype(jnp.float32)
    key_three = key_part.reshape(key_count, group_heads, head_size).astype(jnp.float32)
    value_three = value_part.reshape(key_count, group_heads, head_size).astype(jnp.float32)
    scores = jnp.einsum('qhd,khd->hqk', query_three, key_three) * score_scale
    weights = jnp.where(allowed[None], jnp.exp(scores - norm_part.T[:, :, None]), jnp.float32(0.0))
    grad_weights = jnp.einsum('qhd,khd->hqk', grad_three, value_three)
    grad_scores = weights * (grad_weights - offset_part.T[:, :, None]) * score_scale
    weights_low = weights.astype(jnp.bfloat16).astype(jnp.float32)
    grad_low = grad_scores.astype(jnp.bfloat16).astype(jnp.float32)
    grad_query = jnp.einsum('hqk,khd->qhd', grad_low, key_three).reshape(query_count, -1)
    grad_key = jnp.einsum('hqk,qhd->khd', grad_low, query_three).reshape(key_count, -1)
    grad_value = jnp.einsum('hqk,qhd->khd', weights_low, grad_three).reshape(key_count, -1)
    return (grad_query, grad_key, grad_value)

def pair_grads(query_part, grad_part, norm_part, offset_part, key_part, value_part, allowed, wanted):
    head_count = norm_part.shape[1]
    per_group = math.gcd(head_count, 4)
    groups = head_count // per_group

    def split_heads(source):
        return jnp.moveaxis(source.reshape(source.shape[0], groups, -1), 1, 0)

    def run_group(pieces):
        return group_grads(pieces[0], pieces[1], pieces[2], pieces[3], pieces[4], pieces[5], allowed, wanted)
    results = lax.map(run_group, (split_heads(query_part), split_heads(grad_part), split_heads(norm_part), split_heads(offset_part), split_heads(key_part), split_heads(value_part)))
    return tuple((jnp.moveaxis(result, 0, 1).reshape(result.shape[1], -1) for result in results))

def reference(query_rows, key_rows, value_rows, grad_out, log_norm, grad_offset, listed):
    features = HEADS * D_HEAD
    radius = TC // 2
    blocks = N_ROW * N_COL
    pool_scale = 1.0 / math.sqrt(TR * TC)
    window_rows = TR + 2 * radius
    window_columns = TC + 2 * radius
    limits = (TR * N_ROW, TC * N_COL)

    def pooled(source):
        summed = lax.optimization_barrier(jnp.sum(source.astype(jnp.float32).reshape(N_ROW, TR, N_COL, TC, features), axis=(1, 3)))
        return (summed * pool_scale).reshape(blocks, features).astype(jnp.bfloat16)
    key_summary = pooled(key_rows)
    value_summary = pooled(value_rows)
    margin = ((radius, radius), (radius, radius), (0, 0))
    key_padded = jnp.pad(key_rows, margin)
    value_padded = jnp.pad(value_rows, margin)
    zero_index = jnp.zeros((), jnp.int32)

    def tile_step(state_now, block_id):
        key_total, value_total, summary_table = state_now
        row_start = (block_id // N_COL * TR).astype(jnp.int32)
        column_start = (block_id % N_COL * TC).astype(jnp.int32)
        corner = (row_start, column_start, zero_index)

        def tile_slice(source):
            return lax.dynamic_slice(source, corner, (TR, TC, source.shape[2])).reshape(TR * TC, -1)
        query_tile = tile_slice(query_rows)
        grad_tile = tile_slice(grad_out)
        norm_tile = tile_slice(log_norm)
        offset_tile = tile_slice(grad_offset)
        key_window = lax.dynamic_slice(key_padded, corner, (window_rows, window_columns, features)).reshape(-1, features)
        value_window = lax.dynamic_slice(value_padded, corner, (window_rows, window_columns, features)).reshape(-1, features)
        allowed = window_mask(grid_coords(row_start, column_start, TR, TC), grid_coords(row_start - radius, column_start - radius, window_rows, window_columns), radius, limits)
        grad_query, grad_key, grad_value = pair_grads(query_tile, grad_tile, norm_tile, offset_tile, key_window, value_window, allowed, 'all')
        chosen = listed[block_id]
        extra_query, extra_key, extra_value = pair_grads(query_tile, grad_tile, norm_tile, offset_tile, key_summary[chosen], value_summary[chosen], jnp.ones((TR * TC, SEL), jnp.bool_), 'all')
        shape_window = (window_rows, window_columns, features)
        key_total = lax.dynamic_update_slice(key_total, lax.dynamic_slice(key_total, corner, shape_window) + grad_key.reshape(shape_window), corner)
        value_total = lax.dynamic_update_slice(value_total, lax.dynamic_slice(value_total, corner, shape_window) + grad_value.reshape(shape_window), corner)
        summary_table = summary_table.at[chosen].add(jnp.concatenate([extra_key, extra_value], axis=1))
        return ((key_total, value_total, summary_table), grad_query + extra_query)
    start_state = (jnp.zeros(key_padded.shape, jnp.float32), jnp.zeros(value_padded.shape, jnp.float32), jnp.zeros((blocks, 2 * features), jnp.float32))
    final_state, query_tiles = lax.scan(tile_step, start_state, jnp.arange(blocks, dtype=jnp.int32))
    key_total, value_total, summary_table = final_state
    grad_query = query_tiles.reshape(N_ROW, N_COL, TR, TC, features).transpose(0, 2, 1, 3, 4).reshape(limits[0], limits[1], features)

    def spread(partial_value):
        block_grid = partial_value.reshape(N_ROW, 1, N_COL, 1, features) * pool_scale
        return jnp.broadcast_to(block_grid, (N_ROW, TR, N_COL, TC, features)).reshape(limits[0], limits[1], features)
    grad_key = key_total[radius:radius + limits[0], radius:radius + limits[1]] + spread(summary_table[:, :features])
    grad_value = value_total[radius:radius + limits[0], radius:radius + limits[1]] + spread(summary_table[:, features:])
    return (grad_query, grad_key, grad_value)
```

```python
import math

import jax
import jax.numpy as jnp
from jax import lax
from jax.experimental import pallas as pl
from jax.experimental.pallas import tpu as pltpu
from jax.sharding import PartitionSpec as P

MESH = pl.DeviceIdType.MESH
F32 = jnp.float32
BF16 = jnp.bfloat16
LOG2E = math.log2(math.e)
SCALE = 1.0 / math.sqrt(128)
POOL = 1.0 / math.sqrt(128)
OFF = -1e30
NT = (((1,), (1,)), ((), ()))
TN = (((0,), (0,)), ((), ()))
NEAR = ((-1, 0), (1, 0), (0, -1), (0, 1), (-1, -1), (-1, 1), (1, -1), (1, 1))


def each(low, high, body):
    def step(i, carry):
        body(i)
        return carry

    lax.fori_loop(low, high, step, 0)


def pair_tile(kv, qg, norm, offset, bias):
    both = lax.dot_general(kv, qg, NT, preferred_element_type=F32)
    weights = jnp.exp2(both[:, :128] * (SCALE * LOG2E) - norm + bias)
    grads = weights * (both[:, 128:] - offset) * SCALE
    low = jnp.concatenate([grads.astype(BF16), weights.astype(BF16)], axis=1)
    grad_kv = jnp.dot(low, qg, preferred_element_type=F32)
    grad_q = lax.dot_general(low[:, :128], kv[:, :128], TN, preferred_element_type=F32)
    return grad_kv, grad_q


def kernel(
    q, k, v, go, side_in,
    gq_out, gkv_out, sg_out,
    own, side_src, side, qg, kv_land, kv, acc, gq_acc, gq_low, gkv_low,
    grad_src, grad_ud, grad_lr, win_bias, sum_bias, rows, table, tab, sum_acc, ry, rz, ry_sum, sg_src,
    ld_s, loc_s, side_ss, side_rs, in_ss, in_rs, halo_ss, halo_rs, gh_ss, gh_rs,
    za_ss, za_rs, ya_ss, ya_rs, ry_ss, ry_rs, rz_ss, rz_rs, oq_ss, oq_rs, ok_ss, ok_rs, sg_ss, sg_rs, out_s,
    from_up, from_down,
):
    row, col = lax.axis_index("row"), lax.axis_index("col")
    z, y = row // 2, col // 4
    me = lax.rem(row, 2) * 4 + lax.rem(col, 4)

    def ring(j):
        return (2 * z + j // 4, 4 * y + lax.rem(j, 4))

    def patch(dz, dy):
        return (row + 2 * dz, col + 4 * dy)

    def exists(dz, dy):
        ok = None
        for at, d, n in ((z, dz, 8), (y, dy, 4)):
            if d:
                here = (at > 0) if d < 0 else (at < n - 1)
                ok = here if ok is None else ok & here
        return ok

    def remote(src, dst, ss, rs, device):
        return pltpu.make_async_remote_copy(
            src_ref=src, dst_ref=dst, send_sem=ss, recv_sem=rs, device_id=device, device_id_type=MESH
        )

    barrier = pltpu.get_barrier_semaphore()

    def hello(device):
        pl.semaphore_signal(barrier, inc=1, device_id=device, device_id_type=MESH)

    each(1, 8, lambda o: hello(ring(lax.rem(me + o, 8))))
    each(1, 4, lambda o: hello((row, lax.rem(col + 4 * o, 16))))
    expected = jnp.int32(10)
    for dz, dy in NEAR:
        if dz:
            pl.when(exists(dz, dy))(lambda dz=dz, dy=dy: hello(patch(dz, dy)))
            expected = expected + jnp.where(exists(dz, dy), 1, 0)

    own_k = pltpu.make_async_copy(k, own.at[0], ld_s.at[0])
    own_v = pltpu.make_async_copy(v, own.at[1], ld_s.at[1])
    own_k.start()
    own_v.start()

    def local_in(s, i):
        src = (k, v, q, go)[i].at[:, pl.ds(pl.multiple_of(me * 256 + s * 128, 128), 128)]
        return pltpu.make_async_copy(src, in_dst(s, i, me), loc_s.at[s, i])

    def in_dst(s, i, slot):
        if i < 2:
            return kv_land.at[s, slot, :, pl.ds(128 * i, 128)]
        return qg.at[s, slot, pl.ds(128 * (i - 2), 128), pl.ds(128 * (i - 2), 128)]

    def d_in(s, i, o, slot):
        j = lax.rem(me + o, 8)
        src = (k, v, q, go)[i].at[:, pl.ds(pl.multiple_of(j * 256 + s * 128, 128), 128)]
        return remote(src, in_dst(s, i, slot), in_ss.at[s, i, o], in_rs.at[s, i, o], ring(j))

    for s in range(2):
        for i in range(4):
            local_in(s, i).start()

    def zero_qg(t):
        for s in range(2):
            qg[s, t, 0:128, 128:256] = jnp.zeros((128, 128), BF16)
            qg[s, t, 128:256, 0:128] = jnp.zeros((128, 128), BF16)

    each(0, 8, zero_qg)

    def zero_acc(i):
        for s in range(2):
            for b in range(4):
                acc[s, b, pl.ds(pl.multiple_of(i * 128, 128), 128), :] = jnp.zeros((128, 256), F32)

    each(0, 5, zero_acc)
    for s in range(2):
        sum_acc[s] = jnp.zeros((256, 256), F32)

    @pl.when(z == 0)
    def _():
        for s in range(2):
            kv[s, 0] = jnp.zeros((640, 256), BF16)
            grad_ud[s, 0] = jnp.zeros((640, 256), BF16)

    @pl.when(z == 7)
    def _():
        for s in range(2):
            kv[s, 3] = jnp.zeros((640, 256), BF16)
            grad_ud[s, 1] = jnp.zeros((640, 256), BF16)

    @pl.when(y == 0)
    def _():
        for s in range(2):
            for b in range(4):
                kv[s, b, 0:64] = jnp.zeros((64, 256), BF16)
            for a in range(2):
                grad_lr[s, 0, a] = jnp.zeros((64, 256), BF16)
                grad_ud[s, a, 512:576] = jnp.zeros((64, 256), BF16)

    @pl.when(y == 3)
    def _():
        for s in range(2):
            for b in range(4):
                kv[s, b, 576:640] = jnp.zeros((64, 256), BF16)
            for a in range(2):
                grad_lr[s, 1, a] = jnp.zeros((64, 256), BF16)
                grad_ud[s, a, 576:640] = jnp.zeros((64, 256), BF16)

    key_at = lax.broadcasted_iota(jnp.int32, (256, 128), 0)
    query_at = lax.broadcasted_iota(jnp.int32, (256, 128), 1)
    dc = 8 * (key_at // 64 - 1) + key_at % 8 - query_at % 16
    for j in range(3):
        dr = 8 * (j - 1) + (key_at % 64) // 8 - query_at // 16
        near = (jnp.abs(dr) <= 8) & (jnp.abs(dc) <= 8)
        win_bias[j] = jnp.where(near, F32(0), F32(OFF))

    own_k.wait()
    own_v.wait()
    for j in range(8):
        side_src[j, 0:8] = side_in[j]
        side_src[j, 8:16] = jnp.zeros((8, 128), F32)
        for i in range(2):
            total = jnp.sum(own[i, :, 256 * j : 256 * j + 256].astype(F32), axis=0, keepdims=True)
            total = (total * POOL).astype(BF16).astype(F32)
            side_src[j, 8 + i : 9 + i] = total[:, :128]
            side_src[j, 10 + i : 11 + i] = total[:, 128:]

    pl.semaphore_wait(barrier, expected)

    def d_side(o, slot):
        j = lax.rem(me + o, 8)
        return remote(side_src.at[j], side.at[slot], side_ss.at[o], side_rs.at[o], ring(j))

    each(1, 8, lambda o: d_side(o, me).start())

    def start_in(s, first):
        def body(o):
            d_in(s, first, o, me).start()
            d_in(s, first + 1, o, me).start()

        each(1, 8, body)

    def wait_in(s, first):
        def body(o):
            slot = lax.rem(me + 8 - o, 8)
            d_in(s, first, o, slot).wait_recv()
            d_in(s, first + 1, o, slot).wait_recv()

        each(1, 8, body)
        local_in(s, first).wait()
        local_in(s, first + 1).wait()

    start_in(0, 0)
    start_in(0, 2)

    def relay(_):
        @pl.when(z > 0)
        def _():
            pl.semaphore_signal(from_down, inc=1, device_id=patch(-1, 0), device_id_type=MESH)

        @pl.when(z < 7)
        def _():
            pl.semaphore_signal(from_up, inc=1, device_id=patch(1, 0), device_id_type=MESH)

        @pl.when(z > 0)
        def _():
            pl.semaphore_wait(from_up, 1)

        @pl.when(z < 7)
        def _():
            pl.semaphore_wait(from_down, 1)

    each(0, 6, relay)

    side[me] = side_src[me]
    each(1, 8, lambda o: d_side(o, lax.rem(me + 8 - o, 8)).wait_recv())
    for t in range(8):
        for s in range(2):
            for i in range(2):
                rows[8 * s + t : 8 * s + t + 1, 128 * i : 128 * i + 128] = side[t, 8 + 2 * s + i : 9 + 2 * s + i]
    table[y, z] = rows[...].astype(BF16)

    def d_za(o, slot):
        device = (lax.rem(row + 2 * o, 16), col)
        return remote(table.at[y, z], table.at[y, slot], za_ss.at[o], za_rs.at[o], device)

    each(1, 8, lambda o: d_za(o, z).start())

    def d_ya(o, slot):
        device = (row, lax.rem(col + 4 * o, 16))
        return remote(table.at[y], table.at[slot], ya_ss.at[o], ya_rs.at[o], device)

    def split(s):
        def body(t):
            block = kv_land[s, t].astype(F32).reshape(8, 16, 256)
            base = pl.multiple_of(64 + 128 * lax.rem(t, 4), 64)
            for h in range(2):
                half = block[:, 8 * h : 8 * h + 8].reshape(64, 256).astype(BF16)
                kv[s, 1 + t // 4, pl.ds(pl.multiple_of(base + 64 * h, 64), 64), :] = half

        each(0, 8, body)

    def d_halo(s, n):
        dz, dy = NEAR[n]
        bands = {-1: 1, 1: 2}.get(dz)
        to_bands = {-1: 3, 1: 0}.get(dz)
        at, to = {0: (64, 64), -1: (64, 576), 1: (512, 0)}[dy]
        size = 64 if dy else 512
        if dz:
            src, dst = kv.at[s, bands, pl.ds(at, size)], kv.at[s, to_bands, pl.ds(to, size)]
        else:
            src, dst = kv.at[s, pl.ds(1, 2), pl.ds(at, size)], kv.at[s, pl.ds(1, 2), pl.ds(to, size)]
        return remote(src, dst, halo_ss.at[s, n], halo_rs.at[s, n], patch(dz, dy))

    def start_halo(s):
        for n, (dz, dy) in enumerate(NEAR):
            pl.when(exists(dz, dy))(lambda n=n: d_halo(s, n).start())

    def wait_halo(s):
        for n, (dz, dy) in enumerate(NEAR):
            pl.when(exists(-dz, -dy))(lambda n=n: d_halo(s, n).wait_recv())

    def d_grad(s, n):
        dz, dy = NEAR[n]
        band = {-1: 0, 1: 3}.get(dz)
        at, size = {0: (64, 512), -1: (0, 64), 1: (576, 64)}[dy]
        if dz:
            src = grad_src.at[s, band, pl.ds(at, size)]
            side_at = 1 if dz < 0 else 0
            to = {0: 0, -1: 576, 1: 512}[dy]
            dst = grad_ud.at[s, side_at, pl.ds(to, size)]
        else:
            src = grad_src.at[s, pl.ds(1, 2), pl.ds(at, size)]
            dst = grad_lr.at[s, 1 if dy < 0 else 0]
        return remote(src, dst, gh_ss.at[s, n], gh_rs.at[s, n], patch(dz, dy))

    def start_grad(s):
        for band in (0, 3):
            grad_src[s, band] = acc[s, band].astype(BF16)
        for band in (1, 2):
            for at in (0, 576):
                grad_src[s, band, at : at + 64] = acc[s, band, at : at + 64].astype(BF16)
        for n, (dz, dy) in enumerate(NEAR):
            pl.when(exists(dz, dy))(lambda n=n: d_grad(s, n).start())

    def wait_grad(s):
        for n, (dz, dy) in enumerate(NEAR):
            pl.when(exists(-dz, -dy))(lambda n=n: d_grad(s, n).wait_recv())

    def window(s):
        def body(t):
            a, b = t // 4, lax.rem(t, 4)
            keys = pl.ds(pl.multiple_of(128 * b, 128), 256)
            operand = qg[s, t]
            norm, offset = side[t, s : s + 1], side[t, 2 + s : 3 + s]
            for j in range(3):
                grad_kv, grad_q = pair_tile(kv[s, a + j, keys], operand, norm, offset, win_bias[j])
                acc[s, a + j, keys] = acc[s, a + j, keys] + grad_kv
                total = grad_q if j == 0 else total + grad_q
            return total

        return body

    def summary(s):
        def body(t):
            norm, offset = side[t, s : s + 1], side[t, 2 + s : 3 + s]
            grad_kv, grad_q = pair_tile(tab[s], qg[s, t], norm, offset, sum_bias[t])
            sum_acc[s] = sum_acc[s] + grad_kv
            return grad_q

        return body

    def summary_bias(t):
        at = lax.broadcasted_iota(jnp.int32, (256, 128), 0)
        number = (2 * ((at // 8) % 8) + (at % 8) // 4) * 16 + 4 * (at // 64) + at % 4
        hit = jnp.where(number.astype(F32) == side[t, 4:5], F32(0), F32(OFF))
        sum_bias[t] = jnp.broadcast_to(jnp.max(hit, axis=1, keepdims=True), (256, 128))

    def d_ry(s, o, slot):
        to = lax.rem(y + o, 4)
        src = sum_acc.at[s, pl.ds(pl.multiple_of(64 * to, 64), 64)]
        return remote(src, ry.at[s, slot], ry_ss.at[s, o], ry_rs.at[s, o], (row, lax.rem(col + 4 * o, 16)))

    def d_rz(s, o, slot):
        to = lax.rem(z + o, 8)
        src = ry_sum.at[s, to]
        return remote(src, rz.at[s, slot], rz_ss.at[s, o], rz_rs.at[s, o], (lax.rem(row + 2 * o, 16), col))

    def start_ry(s):
        each(1, 4, lambda o: d_ry(s, o, y).start())

    def mid_reduce(s):
        each(1, 4, lambda o: d_ry(s, o, lax.rem(y + 4 - o, 4)).wait_recv())
        total = sum_acc[s, pl.ds(pl.multiple_of(64 * y, 64), 64), :]
        ry[s, y] = total
        total = (ry[s, 0] + ry[s, 1]) + (ry[s, 2] + ry[s, 3])
        ry_sum[s] = total.reshape(8, 8, 256)
        each(1, 8, lambda o: d_rz(s, o, z).start())

    def end_reduce(s):
        rz[s, z] = ry_sum[s, z]
        each(1, 8, lambda o: d_rz(s, o, lax.rem(z + 8 - o, 8)).wait_recv())
        total = rz[s, 0]
        for n in range(1, 8):
            total = total + rz[s, n]
        total = total * POOL
        for t in range(8):
            sg_src[t, s] = jnp.broadcast_to(total[t : t + 1], (8, 256))

    def d_oq(s, o, slot):
        j = lax.rem(me + o, 8)
        dst = gq_out.at[:, pl.ds(pl.multiple_of(slot * 256 + s * 128, 128), 128)]
        return remote(gq_low.at[s, j], dst, oq_ss.at[s, o], oq_rs.at[s, o], ring(j))

    def l_oq(s):
        dst = gq_out.at[:, pl.ds(pl.multiple_of(me * 256 + s * 128, 128), 128)]
        return pltpu.make_async_copy(gq_low.at[s, me], dst, out_s.at[s])

    def d_ok(s, o, slot):
        j = lax.rem(me + o, 8)
        return remote(gkv_low.at[s, j], gkv_out.at[2 * slot + s], ok_ss.at[s, o], ok_rs.at[s, o], ring(j))

    def l_ok(s):
        return pltpu.make_async_copy(gkv_low.at[s, me], gkv_out.at[2 * me + s], out_s.at[2 + s])

    def d_sg(o, slot):
        j = lax.rem(me + o, 8)
        return remote(sg_src.at[j], sg_out.at[slot], sg_ss.at[o], sg_rs.at[o], ring(j))

    l_sg = pltpu.make_async_copy(sg_src.at[me], sg_out.at[me], out_s.at[4])

    def start_oq(s):
        each(1, 8, lambda o: d_oq(s, o, me).start())
        l_oq(s).start()

    def combine(s):
        def body(t):
            a, b = t // 4, lax.rem(t, 4)
            total = acc[s, 1 + a, pl.ds(pl.multiple_of(64 + 128 * b, 64), 128), :]
            total = total + grad_ud[s, a, pl.ds(pl.multiple_of(128 * b, 128), 128), :].astype(F32)
            left = grad_lr[s, 0, a].astype(F32) + grad_ud[s, a, 512:576].astype(F32)
            right = grad_lr[s, 1, a].astype(F32) + grad_ud[s, a, 576:640].astype(F32)
            none = jnp.zeros((64, 256), F32)
            left = jnp.where(b == 0, left, none)
            right = jnp.where(b == 3, right, none)
            gkv_low[s, t] = (total + jnp.concatenate([left, right], axis=0)).astype(BF16)

        each(0, 8, body)
        each(1, 8, lambda o: d_ok(s, o, me).start())
        l_ok(s).start()

    wait_in(0, 0)
    start_in(1, 0)
    split(0)
    start_halo(0)

    each(0, 8, summary_bias)
    each(1, 8, lambda o: d_za(o, lax.rem(z + 8 - o, 8)).wait_recv())
    each(1, 4, lambda o: d_ya(o, y).start())

    wait_in(0, 2)
    start_in(1, 2)
    wait_halo(0)
    window_0 = window(0)

    def first(t):
        gq_acc[t] = window_0(t)

    each(0, 8, first)
    start_grad(0)

    each(1, 4, lambda o: d_ya(o, lax.rem(y + 4 - o, 4)).wait_recv())
    for s in range(2):
        for n in range(4):
            part = table[n].astype(F32)[:, 8 * s : 8 * s + 8]
            tab[s, 64 * n : 64 * n + 64] = part.reshape(64, 256).astype(BF16)
    summary_0 = summary(0)

    def second(t):
        gq_low[0, t] = (gq_acc[t] + summary_0(t)).astype(BF16)

    each(0, 8, second)
    start_ry(0)
    start_oq(0)

    wait_in(1, 0)
    split(1)
    start_halo(1)
    mid_reduce(0)
    wait_grad(0)
    combine(0)

    wait_in(1, 2)
    summary_1 = summary(1)

    def third(t):
        gq_acc[t] = summary_1(t)

    each(0, 8, third)
    start_ry(1)
    wait_halo(1)
    window_1 = window(1)

    def fourth(t):
        gq_low[1, t] = (gq_acc[t] + window_1(t)).astype(BF16)

    each(0, 8, fourth)
    start_grad(1)
    start_oq(1)
    mid_reduce(1)
    end_reduce(0)
    wait_grad(1)
    combine(1)
    end_reduce(1)
    each(1, 8, lambda o: d_sg(o, me).start())
    l_sg.start()

    def drain_ring(o):
        slot = lax.rem(me + 8 - o, 8)
        d_side(o, me).wait_send()
        d_za(o, z).wait_send()
        for s in range(2):
            for i in range(4):
                d_in(s, i, o, me).wait_send()
            d_rz(s, o, z).wait_send()
            d_oq(s, o, me).wait_send()
            d_oq(s, o, slot).wait_recv()
            d_ok(s, o, me).wait_send()
            d_ok(s, o, slot).wait_recv()
        d_sg(o, me).wait_send()
        d_sg(o, slot).wait_recv()

    each(1, 8, drain_ring)

    def drain_y(o):
        d_ya(o, y).wait_send()
        for s in range(2):
            d_ry(s, o, y).wait_send()

    each(1, 4, drain_y)
    for s in range(2):
        l_oq(s).wait()
        l_ok(s).wait()
        for n, (dz, dy) in enumerate(NEAR):

            def drain_near(n=n, s=s):
                d_halo(s, n).wait_send()
                d_grad(s, n).wait_send()

            pl.when(exists(dz, dy))(drain_near)
    l_sg.wait()


def finish(gq, gkv, sg, out_q, out_k, out_v):
    heads = gkv.shape[0]
    out_q[...] = gq[...].astype(F32).reshape(out_q.shape)
    for n in range(heads):
        total = gkv[n].astype(F32) + sg[n // 2, n % 2, 0:1]
        for h in range(2):
            half = total[64 * h : 64 * h + 64]
            out_k[:, 8 * h : 8 * h + 8, 128 * n : 128 * n + 128] = half[:, :128].reshape(8, 8, 128)
            out_v[:, 8 * h : 8 * h + 8, 128 * n : 128 * n + 128] = half[:, 128:].reshape(8, 8, 128)


def on_device(query_rows, key_rows, value_rows, grad_out, log_norm, grad_offset, listed):
    flat = [x.reshape(128, 2048) for x in (query_rows, key_rows, value_rows, grad_out)]
    norm = (log_norm.reshape(128, 16) * LOG2E).T.reshape(8, 2, 128)
    offset = grad_offset.reshape(128, 16).T.reshape(8, 2, 128)
    names = jnp.pad(listed.astype(F32), ((0, 0), (0, 64)), constant_values=-1.0)
    names = jnp.broadcast_to(names[None], (8, 4, 128))
    side = jnp.concatenate([norm, offset, names], axis=1)
    dma = pltpu.SemaphoreType.DMA
    gq, gkv, sg = pl.pallas_call(
        kernel,
        out_shape=(
            jax.ShapeDtypeStruct((128, 2048), BF16),
            jax.ShapeDtypeStruct((16, 128, 256), BF16),
            jax.ShapeDtypeStruct((8, 2, 8, 256), F32),
        ),
        in_specs=[pl.BlockSpec(memory_space=pl.ANY)] * 4 + [pl.BlockSpec(memory_space=pltpu.VMEM)],
        out_specs=(pl.BlockSpec(memory_space=pl.ANY),) * 3,
        scratch_shapes=[
            pltpu.VMEM((2, 128, 2048), BF16),
            pltpu.VMEM((8, 16, 128), F32),
            pltpu.VMEM((8, 16, 128), F32),
            pltpu.VMEM((2, 8, 256, 256), BF16),
            pltpu.VMEM((2, 8, 128, 256), BF16),
            pltpu.VMEM((2, 4, 640, 256), BF16),
            pltpu.VMEM((2, 4, 640, 256), F32),
            pltpu.VMEM((8, 128, 128), F32),
            pltpu.VMEM((2, 8, 128, 128), BF16),
            pltpu.VMEM((2, 8, 128, 256), BF16),
            pltpu.VMEM((2, 4, 640, 256), BF16),
            pltpu.VMEM((2, 2, 640, 256), BF16),
            pltpu.VMEM((2, 2, 2, 64, 256), BF16),
            pltpu.VMEM((3, 256, 128), F32),
            pltpu.VMEM((8, 256, 128), F32),
            pltpu.VMEM((16, 256), F32),
            pltpu.VMEM((4, 8, 16, 256), BF16),
            pltpu.VMEM((2, 256, 256), BF16),
            pltpu.VMEM((2, 256, 256), F32),
            pltpu.VMEM((2, 4, 64, 256), F32),
            pltpu.VMEM((2, 8, 8, 256), F32),
            pltpu.VMEM((2, 8, 8, 256), F32),
            pltpu.VMEM((8, 2, 8, 256), F32),
            dma((2,)), dma((2, 4)), dma((8,)), dma((8,)), dma((2, 4, 8)), dma((2, 4, 8)),
            dma((2, 8)), dma((2, 8)), dma((2, 8)), dma((2, 8)),
            dma((8,)), dma((8,)), dma((4,)), dma((4,)), dma((2, 4)), dma((2, 4)), dma((2, 8)), dma((2, 8)),
            dma((2, 8)), dma((2, 8)), dma((2, 8)), dma((2, 8)), dma((8,)), dma((8,)), dma((5,)),
            pltpu.SemaphoreType.REGULAR, pltpu.SemaphoreType.REGULAR,
        ],
        compiler_params=pltpu.CompilerParams(
            collective_id=0, has_side_effects=True, vmem_limit_bytes=48 * 2**20
        ),
        name="exchange",
    )(*flat, side)
    steps = 4
    heads = 16 // steps
    wide = heads * 128
    return pl.pallas_call(
        finish,
        grid=(steps,),
        out_shape=(jax.ShapeDtypeStruct((8, 16, 2048), F32),) * 3,
        in_specs=[
            pl.BlockSpec((128, wide), lambda i: (0, i)),
            pl.BlockSpec((heads, 128, 256), lambda i: (i, 0, 0)),
            pl.BlockSpec((heads // 2, 2, 8, 256), lambda i: (i, 0, 0, 0)),
        ],
        out_specs=(pl.BlockSpec((8, 16, wide), lambda i: (0, 0, i)),) * 3,
        compiler_params=pltpu.CompilerParams(vmem_limit_bytes=32 * 2**20),
        name="finish",
    )(gq, gkv, sg)


def solution(mesh):
    tokens = P("row", "col", None)
    return jax.shard_map(
        on_device,
        mesh=mesh,
        in_specs=(tokens,) * 6 + (P(("row", "col"), None),),
        out_specs=(tokens,) * 3,
        check_vma=False,
    )
```

```python
import math

import jax
import jax.numpy as jnp
from jax import lax
from jax.experimental import pallas as pl
from jax.experimental.pallas import tpu as pltpu
from jax.sharding import PartitionSpec as P

MESH = pl.DeviceIdType.MESH
F32 = jnp.float32
BF16 = jnp.bfloat16
LOG2E = math.log2(math.e)
SCALE = 1.0 / math.sqrt(128)
POOL = 1.0 / math.sqrt(128)
OFF = -1e30
NT = (((1,), (1,)), ((), ()))
TN = (((0,), (0,)), ((), ()))
NEAR = ((-1, 0), (1, 0), (0, -1), (0, 1), (-1, -1), (-1, 1), (1, -1), (1, 1))


def each(low, high, body):
    def step(i, carry):
        body(i)
        return carry

    lax.fori_loop(low, high, step, 0)


def pair_tile(qg, keys, values, norm, offset, bias):
    q, go = qg[:, :128], qg[:, 128:]
    scores = lax.dot_general(q, keys, NT, preferred_element_type=F32)
    grad_weights = lax.dot_general(go, values, NT, preferred_element_type=F32)
    weights = jnp.exp2(scores * (SCALE * LOG2E) - norm + bias)
    grads = (weights * (grad_weights - offset) * SCALE).astype(BF16)
    grad_q = jnp.dot(grads, keys, preferred_element_type=F32)
    grad_k = lax.dot_general(grads, q, TN, preferred_element_type=F32)
    grad_v = lax.dot_general(weights.astype(BF16), go, TN, preferred_element_type=F32)
    return grad_k, grad_v, grad_q


def kernel(
    q, k, v, go, norm_in, offset_in, listed_in,
    gq_out, gkv_out, sg_out,
    own, own_norm, own_listed, side_src, side, side_col, qg_land, qg, kv, lanes, acc, gq_low, gkv_low,
    grad_src, grad_ud, grad_lr, win_bias, sum_bias, rows, table, tab, sum_acc, sum_low, ry, rz, ry_sum, sg_src,
    ld_s, loc_s, side_ss, side_rs, sh_ss, sh_rs, in_ss, in_rs, halo_ss, halo_rs, gh_ss, gh_rs,
    za_ss, za_rs, ya_ss, ya_rs, ry_ss, ry_rs, rz_ss, rz_rs, oq_ss, oq_rs, ok_ss, ok_rs, sg_ss, sg_rs, out_s,
    from_up, from_down,
):
    row, col = lax.axis_index("row"), lax.axis_index("col")
    z, y = row // 2, col // 4
    me = lax.rem(row, 2) * 4 + lax.rem(col, 4)

    def ring(j):
        return (2 * z + j // 4, 4 * y + lax.rem(j, 4))

    def patch(dz, dy):
        return (row + 2 * dz, col + 4 * dy)

    def exists(dz, dy):
        ok = None
        for at, d, n in ((z, dz, 8), (y, dy, 4)):
            if d:
                here = (at > 0) if d < 0 else (at < n - 1)
                ok = here if ok is None else ok & here
        return ok

    def remote(src, dst, ss, rs, device):
        return pltpu.make_async_remote_copy(
            src_ref=src, dst_ref=dst, send_sem=ss, recv_sem=rs, device_id=device, device_id_type=MESH
        )

    barrier = pltpu.get_barrier_semaphore()

    def hello(device):
        pl.semaphore_signal(barrier, inc=1, device_id=device, device_id_type=MESH)

    each(1, 8, lambda o: hello(ring(lax.rem(me + o, 8))))
    each(1, 4, lambda o: hello((row, lax.rem(col + 4 * o, 16))))
    expected = jnp.int32(10)
    for dz, dy in NEAR:
        if dz:
            pl.when(exists(dz, dy))(lambda dz=dz, dy=dy: hello(patch(dz, dy)))
            expected = expected + jnp.where(exists(dz, dy), 1, 0)

    own_k = pltpu.make_async_copy(k, own.at[0], ld_s.at[0])
    own_v = pltpu.make_async_copy(v, own.at[1], ld_s.at[1])
    own_n = pltpu.make_async_copy(norm_in, own_norm.at[0], ld_s.at[2])
    own_o = pltpu.make_async_copy(offset_in, own_norm.at[1], ld_s.at[3])
    own_l = pltpu.make_async_copy(listed_in, own_listed, ld_s.at[4])
    for copy in (own_k, own_v, own_n, own_o, own_l):
        copy.start()

    def local_in(s, i):
        src = (k, v, q, go)[i].at[:, pl.ds(pl.multiple_of(me * 256 + s * 128, 128), 128)]
        return pltpu.make_async_copy(src, in_dst(s, i, me), loc_s.at[s, i])

    def in_dst(s, i, slot):
        if i < 2:
            return kv.at[s, i, slot]
        return qg_land.at[s, slot, :, pl.ds(128 * (i - 2), 128)]

    def d_in(s, i, o, slot):
        j = lax.rem(me + o, 8)
        src = (k, v, q, go)[i].at[:, pl.ds(pl.multiple_of(j * 256 + s * 128, 128), 128)]
        return remote(src, in_dst(s, i, slot), in_ss.at[s, i, o], in_rs.at[s, i, o], ring(j))

    for s in range(2):
        for i in range(4):
            local_in(s, i).start()

    def zero_acc(i):
        for s in range(2):
            for b in range(4):
                acc[s, b, pl.ds(pl.multiple_of(i * 128, 128), 128), :] = jnp.zeros((128, 128), F32)

    each(0, 5, zero_acc)

    for at, end, band, ud in ((z, 0, 0, 0), (z, 7, 3, 1)):

        @pl.when(at == end)
        def _(band=band, ud=ud):
            for b in range(6):
                side[band, b] = jnp.zeros((16, 128), F32)
            for s in range(2):
                qg[s, band] = jnp.zeros((640, 256), BF16)
                grad_ud[s, ud] = jnp.zeros((640, 128), BF16)

    for at, end, first, block, lr, ud in ((y, 0, 0, 0, 0, 512), (y, 3, 576, 5, 1, 576)):

        @pl.when(at == end)
        def _(first=first, block=block, lr=lr, ud=ud):
            for b in range(4):
                side[b, block] = jnp.zeros((16, 128), F32)
            for s in range(2):
                for b in range(4):
                    qg[s, b, first : first + 64] = jnp.zeros((64, 256), BF16)
                for a in range(2):
                    grad_lr[s, lr, a] = jnp.zeros((64, 128), BF16)
                    grad_ud[s, a, ud : ud + 64] = jnp.zeros((64, 128), BF16)

    query_at = lax.broadcasted_iota(jnp.int32, (256, 128), 0)
    key_at = lax.broadcasted_iota(jnp.int32, (256, 128), 1)
    dc = 8 * (query_at // 64 - 1) + query_at % 8 - key_at % 16
    for j in range(3):
        dr = 8 * (j - 1) + (query_at % 64) // 8 - key_at // 16
        near = (jnp.abs(dr) <= 8) & (jnp.abs(dc) <= 8)
        win_bias[j] = jnp.where(near, F32(0), F32(OFF))

    for copy in (own_k, own_v, own_n, own_o, own_l):
        copy.wait()
    norm = own_norm[0].T * LOG2E
    offset = own_norm[1].T
    for j in range(8):
        side_src[j] = jnp.zeros((16, 128), F32)
        side_src[j, 0:2] = norm[2 * j : 2 * j + 2]
        side_src[j, 2:4] = offset[2 * j : 2 * j + 2]
        side_src[j, 4:5, 0:64] = own_listed[...].astype(F32)
        for i in range(2):
            total = jnp.sum(own[i, :, 256 * j : 256 * j + 256].astype(F32), axis=0, keepdims=True)
            total = (total * POOL).astype(BF16).astype(F32)
            side_src[j, 8 + i : 9 + i] = total[:, :128]
            side_src[j, 10 + i : 11 + i] = total[:, 128:]

    pl.semaphore_wait(barrier, expected)

    def d_side(o, slot):
        j = lax.rem(me + o, 8)
        dst = side.at[1 + slot // 4, 1 + lax.rem(slot, 4)]
        return remote(side_src.at[j], dst, side_ss.at[o], side_rs.at[o], ring(j))

    each(1, 8, lambda o: d_side(o, me).start())

    def start_in(s, first):
        def body(o):
            d_in(s, first, o, me).start()
            d_in(s, first + 1, o, me).start()

        each(1, 8, body)

    def wait_in(s, first):
        def body(o):
            slot = lax.rem(me + 8 - o, 8)
            d_in(s, first, o, slot).wait_recv()
            d_in(s, first + 1, o, slot).wait_recv()

        each(1, 8, body)
        local_in(s, first).wait()
        local_in(s, first + 1).wait()


    batches = [(0, 2), (1, 2), (0, 0), (1, 0)]
    for n in range(6):

        @pl.when(z > 0)
        def _():
            pl.semaphore_signal(from_down, inc=1, device_id=patch(-1, 0), device_id_type=MESH)

        @pl.when(z < 7)
        def _():
            pl.semaphore_signal(from_up, inc=1, device_id=patch(1, 0), device_id_type=MESH)

        if n < 4:
            start_in(*batches[n])

        @pl.when(z > 0)
        def _():
            pl.semaphore_wait(from_up, 1)

        @pl.when(z < 7)
        def _():
            pl.semaphore_wait(from_down, 1)

    side[1 + me // 4, 1 + lax.rem(me, 4)] = side_src[me]
    each(1, 8, lambda o: d_side(o, lax.rem(me + 8 - o, 8)).wait_recv())
    for t in range(8):
        for s in range(2):
            for i in range(2):
                one = side[1 + t // 4, 1 + t % 4, 8 + 2 * s + i : 9 + 2 * s + i]
                rows[8 * s + t : 8 * s + t + 1, 128 * i : 128 * i + 128] = one
    table[y, z] = rows[...].astype(BF16)

    def d_za(o, slot):
        device = (lax.rem(row + 2 * o, 16), col)
        return remote(table.at[y, z], table.at[y, slot], za_ss.at[o], za_rs.at[o], device)

    each(1, 8, lambda o: d_za(o, z).start())

    def d_ya(o, slot):
        device = (row, lax.rem(col + 4 * o, 16))
        return remote(table.at[y], table.at[slot], ya_ss.at[o], ya_rs.at[o], device)

    def split(s):
        def body(t):
            block = qg_land[s, t].astype(F32).reshape(8, 16, 256)
            base = pl.multiple_of(64 + 128 * lax.rem(t, 4), 64)
            for h in range(2):
                half = block[:, 8 * h : 8 * h + 8].reshape(64, 256).astype(BF16)
                qg[s, 1 + t // 4, pl.ds(pl.multiple_of(base + 64 * h, 64), 64), :] = half

        each(0, 8, body)

    def d_halo(s, n):
        dz, dy = NEAR[n]
        band, to_band = {-1: 1, 1: 2}.get(dz), {-1: 3, 1: 0}.get(dz)
        at, to = {0: (64, 64), -1: (64, 576), 1: (512, 0)}[dy]
        size = 64 if dy else 512
        if dz:
            src, dst = qg.at[s, band, pl.ds(at, size)], qg.at[s, to_band, pl.ds(to, size)]
        else:
            src, dst = qg.at[s, pl.ds(1, 2), pl.ds(at, size)], qg.at[s, pl.ds(1, 2), pl.ds(to, size)]
        return remote(src, dst, halo_ss.at[s, n], halo_rs.at[s, n], patch(dz, dy))

    def d_sh(n):
        dz, dy = NEAR[n]
        band, to_band = {-1: 1, 1: 2}.get(dz), {-1: 3, 1: 0}.get(dz)
        at, to = {0: (1, 1), -1: (1, 5), 1: (4, 0)}[dy]
        size = 1 if dy else 4
        if dz:
            src, dst = side.at[band, pl.ds(at, size)], side.at[to_band, pl.ds(to, size)]
        else:
            src, dst = side.at[pl.ds(1, 2), pl.ds(at, size)], side.at[pl.ds(1, 2), pl.ds(to, size)]
        return remote(src, dst, sh_ss.at[n], sh_rs.at[n], patch(dz, dy))

    def start_near(make):
        for n, (dz, dy) in enumerate(NEAR):
            pl.when(exists(dz, dy))(lambda n=n: make(n).start())

    def wait_near(make):
        for n, (dz, dy) in enumerate(NEAR):
            pl.when(exists(-dz, -dy))(lambda n=n: make(n).wait_recv())

    def spread(band, block, halves):
        columns = side[band, block].T
        side_col[...] = columns
        for s in range(2):
            for i in range(2):
                wide = jnp.broadcast_to(columns[:, 2 * i + s : 2 * i + s + 1], (128, 128)).reshape(8, 16, 128)
                for h, at in halves:
                    lanes[s, i, band, pl.ds(at, 64), :] = wide[:, 8 * h : 8 * h + 8].reshape(64, 128)

    def spread_own(t):
        band, block = 1 + t // 4, 1 + lax.rem(t, 4)
        base = 128 * block - 64
        spread(band, block, ((0, pl.multiple_of(base, 64)), (1, pl.multiple_of(base + 64, 64))))
        at = lax.broadcasted_iota(jnp.int32, (64, 256), 1)
        number = (2 * ((at // 8) % 8) + (at % 8) // 4) * 16 + 4 * (at // 64) + at % 4
        hit = jnp.where(number.astype(F32) == side_col[0:64, 4:5], F32(0), F32(OFF))
        sum_bias[t] = jnp.broadcast_to(jnp.max(hit, axis=0, keepdims=True), (8, 256))

    def spread_halo():
        for band in (0, 3):

            def middle(n, band=band):
                base = 128 * n - 64
                spread(band, n, ((0, pl.multiple_of(base, 64)), (1, pl.multiple_of(base + 64, 64))))

            each(1, 5, middle)

        def edges(band):
            spread(band, 0, ((1, 0),))
            spread(band, 5, ((0, 576),))

        each(0, 4, edges)

    def d_grad(s, n):
        dz, dy = NEAR[n]
        band = {-1: 0, 1: 3}.get(dz)
        at, size = {0: (64, 512), -1: (0, 64), 1: (576, 64)}[dy]
        if dz:
            src = grad_src.at[s, band, pl.ds(at, size)]
            side_at = 1 if dz < 0 else 0
            to = {0: 0, -1: 576, 1: 512}[dy]
            dst = grad_ud.at[s, side_at, pl.ds(to, size)]
        else:
            src = grad_src.at[s, pl.ds(1, 2), pl.ds(at, size)]
            dst = grad_lr.at[s, 1 if dy < 0 else 0]
        return remote(src, dst, gh_ss.at[s, n], gh_rs.at[s, n], patch(dz, dy))

    def start_grad(s):
        for band in (0, 3):
            grad_src[s, band] = acc[s, band].astype(BF16)
        for band in (1, 2):
            for at in (0, 576):
                grad_src[s, band, at : at + 64] = acc[s, band, at : at + 64].astype(BF16)
        start_near(lambda n: d_grad(s, n))

    def compute(s):
        def body(t, carry):
            a, b = t // 4, lax.rem(t, 4)
            queries = pl.ds(pl.multiple_of(128 * b, 128), 256)
            operand = jnp.concatenate([qg[s, a + j, queries] for j in range(3)], axis=0)
            norm = jnp.concatenate([lanes[s, 0, a + j, queries] for j in range(3)], axis=0)
            offset = jnp.concatenate([lanes[s, 1, a + j, queries] for j in range(3)], axis=0)
            bias = jnp.concatenate([win_bias[j] for j in range(3)], axis=0)
            grad_k, grad_v, grad_q = pair_tile(operand, kv[s, 0, t], kv[s, 1, t], norm, offset, bias)
            for j in range(3):
                acc[s, a + j, queries] = acc[s, a + j, queries] + grad_q[256 * j : 256 * j + 256]
            gkv_low[s, t, :, 0:128] = grad_k.astype(BF16)
            gkv_low[s, t, :, 128:256] = grad_v.astype(BF16)
            return carry

        lax.fori_loop(0, 8, body, 0, unroll=4)

    def summary(s):
        keys, values = tab[s, :, 0:128], tab[s, :, 128:256]
        for a in range(2):
            operand = qg[s, 1 + a, 64:576]
            norm, offset = lanes[s, 0, 1 + a, 64:576], lanes[s, 1, 1 + a, 64:576]
            bias = jnp.concatenate(
                [jnp.broadcast_to(sum_bias[4 * a + b, 0:1], (128, 256)) for b in range(4)], axis=0
            )
            grad_k, grad_v, grad_q = pair_tile(
                operand,
                keys,
                values,
                jnp.concatenate([norm, norm], axis=1),
                jnp.concatenate([offset, offset], axis=1),
                bias,
            )
            acc[s, 1 + a, 64:576] = acc[s, 1 + a, 64:576] + grad_q
            sum_acc[s, :, 0:128] = grad_k if a == 0 else sum_acc[s, :, 0:128] + grad_k
            sum_acc[s, :, 128:256] = grad_v if a == 0 else sum_acc[s, :, 128:256] + grad_v

    def d_ry(s, o, slot):
        to = lax.rem(y + o, 4)
        src = sum_low.at[s, pl.ds(pl.multiple_of(64 * to, 64), 64)]
        return remote(src, ry.at[s, slot], ry_ss.at[s, o], ry_rs.at[s, o], (row, lax.rem(col + 4 * o, 16)))

    def d_rz(s, o, slot):
        to = lax.rem(z + o, 8)
        src = ry_sum.at[s, to]
        return remote(src, rz.at[s, slot], rz_ss.at[s, o], rz_rs.at[s, o], (lax.rem(row + 2 * o, 16), col))

    def start_ry(s):
        sum_low[s] = sum_acc[s].astype(BF16)
        each(1, 4, lambda o: d_ry(s, o, y).start())

    def mid_reduce(s):
        each(1, 4, lambda o: d_ry(s, o, lax.rem(y + 4 - o, 4)).wait_recv())
        total = sum_acc[s, pl.ds(pl.multiple_of(64 * y, 64), 64), :]
        ry[s, y] = jnp.zeros((64, 256), BF16)
        for n in range(4):
            total = total + ry[s, n].astype(F32)
        ry_sum[s] = total.reshape(8, 8, 256)
        each(1, 8, lambda o: d_rz(s, o, z).start())

    def end_reduce(s):
        rz[s, z] = ry_sum[s, z]
        each(1, 8, lambda o: d_rz(s, o, lax.rem(z + 8 - o, 8)).wait_recv())
        total = rz[s, 0]
        for n in range(1, 8):
            total = total + rz[s, n]
        total = total * POOL
        for t in range(8):
            sg_src[t, s] = jnp.broadcast_to(total[t : t + 1], (8, 256))

    def d_oq(s, o, slot):
        j = lax.rem(me + o, 8)
        return remote(gq_low.at[s, j], gq_out.at[2 * slot + s], oq_ss.at[s, o], oq_rs.at[s, o], ring(j))

    def l_oq(s):
        return pltpu.make_async_copy(gq_low.at[s, me], gq_out.at[2 * me + s], out_s.at[s])

    def d_ok(s, o, slot):
        j = lax.rem(me + o, 8)
        return remote(gkv_low.at[s, j], gkv_out.at[2 * slot + s], ok_ss.at[s, o], ok_rs.at[s, o], ring(j))

    def l_ok(s):
        return pltpu.make_async_copy(gkv_low.at[s, me], gkv_out.at[2 * me + s], out_s.at[2 + s])

    def d_sg(o, slot):
        j = lax.rem(me + o, 8)
        return remote(sg_src.at[j], sg_out.at[slot], sg_ss.at[o], sg_rs.at[o], ring(j))

    l_sg = pltpu.make_async_copy(sg_src.at[me], sg_out.at[me], out_s.at[4])

    def start_ok(s):
        each(1, 8, lambda o: d_ok(s, o, me).start())
        l_ok(s).start()

    def combine(s):
        def body(t):
            a, b = t // 4, lax.rem(t, 4)
            total = acc[s, 1 + a, pl.ds(pl.multiple_of(64 + 128 * b, 64), 128), :]
            total = total + grad_ud[s, a, pl.ds(pl.multiple_of(128 * b, 128), 128), :].astype(F32)
            left = grad_lr[s, 0, a].astype(F32) + grad_ud[s, a, 512:576].astype(F32)
            right = grad_lr[s, 1, a].astype(F32) + grad_ud[s, a, 576:640].astype(F32)
            none = jnp.zeros((64, 128), F32)
            left = jnp.where(b == 0, left, none)
            right = jnp.where(b == 3, right, none)
            gq_low[s, t] = (total + jnp.concatenate([left, right], axis=0)).astype(BF16)

        each(0, 8, body)
        each(1, 8, lambda o: d_oq(s, o, me).start())
        l_oq(s).start()

    start_near(d_sh)
    for s in range(2):
        wait_in(s, 2)
        split(s)
        start_near(lambda n, s=s: d_halo(s, n))

    each(0, 8, spread_own)
    each(1, 8, lambda o: d_za(o, lax.rem(z + 8 - o, 8)).wait_recv())
    each(1, 4, lambda o: d_ya(o, y).start())
    wait_near(d_sh)
    spread_halo()
    wait_in(0, 0)
    wait_near(lambda n: d_halo(0, n))
    compute(0)
    start_ok(0)
    start_grad(0)
    each(1, 4, lambda o: d_ya(o, lax.rem(y + 4 - o, 4)).wait_recv())
    for s in range(2):
        for n in range(4):
            part = table[n].astype(F32)[:, 8 * s : 8 * s + 8]
            tab[s, 64 * n : 64 * n + 64] = part.reshape(64, 256).astype(BF16)
    for s in range(2):
        summary(s)
        start_ry(s)
    wait_in(1, 0)
    wait_near(lambda n: d_halo(1, n))
    compute(1)
    start_ok(1)
    start_grad(1)
    mid_reduce(0)
    mid_reduce(1)
    for s in range(2):
        wait_near(lambda n, s=s: d_grad(s, n))
        combine(s)
    end_reduce(0)
    end_reduce(1)
    each(1, 8, lambda o: d_sg(o, me).start())
    l_sg.start()

    def drain_ring(o):
        slot = lax.rem(me + 8 - o, 8)
        d_side(o, me).wait_send()
        d_za(o, z).wait_send()
        for s in range(2):
            for i in range(4):
                d_in(s, i, o, me).wait_send()
            d_rz(s, o, z).wait_send()
            d_oq(s, o, me).wait_send()
            d_oq(s, o, slot).wait_recv()
            d_ok(s, o, me).wait_send()
            d_ok(s, o, slot).wait_recv()
        d_sg(o, me).wait_send()
        d_sg(o, slot).wait_recv()

    each(1, 8, drain_ring)

    def drain_y(o):
        d_ya(o, y).wait_send()
        for s in range(2):
            d_ry(s, o, y).wait_send()

    each(1, 4, drain_y)
    for s in range(2):
        l_oq(s).wait()
        l_ok(s).wait()
        for n, (dz, dy) in enumerate(NEAR):

            def drain_near(n=n, s=s):
                d_halo(s, n).wait_send()
                d_grad(s, n).wait_send()
                if s == 0:
                    d_sh(n).wait_send()

            pl.when(exists(dz, dy))(drain_near)
    l_sg.wait()


def finish(gq, gkv, sg, out_q, out_k, out_v):
    heads = gkv.shape[0]
    for n in range(heads):
        total = gkv[n].astype(F32) + sg[n // 2, n % 2, 0:1]
        at = slice(128 * n, 128 * n + 128)
        out_k[:, :, at] = total[:, :128].reshape(8, 16, 128)
        out_v[:, :, at] = total[:, 128:].reshape(8, 16, 128)
        for h in range(2):
            out_q[:, 8 * h : 8 * h + 8, at] = gq[n, 64 * h : 64 * h + 64].astype(F32).reshape(8, 8, 128)


def on_device(query_rows, key_rows, value_rows, grad_out, log_norm, grad_offset, listed):
    flat = [x.reshape(128, 2048) for x in (query_rows, key_rows, value_rows, grad_out)]
    flat += [log_norm.reshape(128, 16), grad_offset.reshape(128, 16), listed]
    dma = pltpu.SemaphoreType.DMA
    gq, gkv, sg = pl.pallas_call(
        kernel,
        out_shape=(
            jax.ShapeDtypeStruct((16, 128, 128), BF16),
            jax.ShapeDtypeStruct((16, 128, 256), BF16),
            jax.ShapeDtypeStruct((8, 2, 8, 256), F32),
        ),
        in_specs=[pl.BlockSpec(memory_space=pltpu.HBM)] * 7,
        out_specs=(pl.BlockSpec(memory_space=pltpu.HBM),) * 3,
        scratch_shapes=[
            pltpu.VMEM((2, 128, 2048), BF16),
            pltpu.VMEM((2, 128, 16), F32),
            pltpu.VMEM((1, 64), jnp.int32),
            pltpu.VMEM((8, 16, 128), F32),
            pltpu.VMEM((4, 6, 16, 128), F32),
            pltpu.VMEM((128, 16), F32),
            pltpu.VMEM((2, 8, 128, 256), BF16),
            pltpu.VMEM((2, 4, 640, 256), BF16),
            pltpu.VMEM((2, 2, 8, 128, 128), BF16),
            pltpu.VMEM((2, 2, 4, 640, 128), F32),
            pltpu.VMEM((2, 4, 640, 128), F32),
            pltpu.VMEM((2, 8, 128, 128), BF16),
            pltpu.VMEM((2, 8, 128, 256), BF16),
            pltpu.VMEM((2, 4, 640, 128), BF16),
            pltpu.VMEM((2, 2, 640, 128), BF16),
            pltpu.VMEM((2, 2, 2, 64, 128), BF16),
            pltpu.VMEM((3, 256, 128), F32),
            pltpu.VMEM((8, 8, 256), F32),
            pltpu.VMEM((16, 256), F32),
            pltpu.VMEM((4, 8, 16, 256), BF16),
            pltpu.VMEM((2, 256, 256), BF16),
            pltpu.VMEM((2, 256, 256), F32),
            pltpu.VMEM((2, 256, 256), BF16),
            pltpu.VMEM((2, 4, 64, 256), BF16),
            pltpu.VMEM((2, 8, 8, 256), F32),
            pltpu.VMEM((2, 8, 8, 256), F32),
            pltpu.VMEM((8, 2, 8, 256), F32),
            dma((5,)), dma((2, 4)), dma((8,)), dma((8,)), dma((8,)), dma((8,)), dma((2, 4, 8)), dma((2, 4, 8)),
            dma((2, 8)), dma((2, 8)), dma((2, 8)), dma((2, 8)),
            dma((8,)), dma((8,)), dma((4,)), dma((4,)), dma((2, 4)), dma((2, 4)), dma((2, 8)), dma((2, 8)),
            dma((2, 8)), dma((2, 8)), dma((2, 8)), dma((2, 8)), dma((8,)), dma((8,)), dma((5,)),
            pltpu.SemaphoreType.REGULAR, pltpu.SemaphoreType.REGULAR,
        ],
        compiler_params=pltpu.CompilerParams(
            collective_id=0, has_side_effects=True, vmem_limit_bytes=60 * 2**20
        ),
        name="exchange",
    )(*flat)
    steps = 4
    heads = 16 // steps
    wide = heads * 128
    return pl.pallas_call(
        finish,
        grid=(steps,),
        out_shape=(jax.ShapeDtypeStruct((8, 16, 2048), F32),) * 3,
        in_specs=[
            pl.BlockSpec((heads, 128, 128), lambda i: (i, 0, 0)),
            pl.BlockSpec((heads, 128, 256), lambda i: (i, 0, 0)),
            pl.BlockSpec((heads // 2, 2, 8, 256), lambda i: (i, 0, 0, 0)),
        ],
        out_specs=(pl.BlockSpec((8, 16, wide), lambda i: (0, 0, i)),) * 3,
        compiler_params=pltpu.CompilerParams(vmem_limit_bytes=60 * 2**20),
        name="finish",
    )(gq, gkv, sg)


def solution(mesh):
    tokens = P("row", "col", None)
    return jax.shard_map(
        on_device,
        mesh=mesh,
        in_specs=(tokens,) * 6 + (P(("row", "col"), None),),
        out_specs=(tokens,) * 3,
        check_vma=False,
    )
```

```python
import math

import jax
import jax.numpy as jnp
from jax import lax
from jax.experimental import pallas as pl
from jax.experimental.pallas import tpu as pltpu
from jax.sharding import PartitionSpec as P

MESH = pl.DeviceIdType.MESH
F32 = jnp.float32
BF16 = jnp.bfloat16
LOG2E = math.log2(math.e)
SCALE = 1.0 / math.sqrt(128)
POOL = 1.0 / math.sqrt(128)
OFF = -1e30
NT = (((1,), (1,)), ((), ()))
TN = (((0,), (0,)), ((), ()))
NEAR = ((-1, 0), (1, 0), (0, -1), (0, 1), (-1, -1), (-1, 1), (1, -1), (1, 1))


def each(low, high, body, unroll=1):
    def step(i, carry):
        body(i)
        return carry

    lax.fori_loop(low, high, step, 0, unroll=unroll)


def pair_tile(qg, keys, values, norm, offset, bias):
    q, go = qg[:, :128], qg[:, 128:]
    scores = lax.dot_general(q, keys, NT, preferred_element_type=F32)
    grad_weights = lax.dot_general(go, values, NT, preferred_element_type=F32)
    weights = jnp.exp2(scores * (SCALE * LOG2E) - norm + bias)
    grads = (weights * (grad_weights - offset) * SCALE).astype(BF16)
    grad_q = jnp.dot(grads, keys, preferred_element_type=F32)
    grad_k = lax.dot_general(grads, q, TN, preferred_element_type=F32)
    grad_v = lax.dot_general(weights.astype(BF16), go, TN, preferred_element_type=F32)
    return grad_k, grad_v, grad_q


def kernel(
    q, k, v, go, norm_in, offset_in, listed_in,
    gq_out, gkv_out, sg_out,
    own, own_norm, own_listed, side_src, side, side_col, qg_land, qg, kv, lanes, acc, gq_low, gkv_low,
    grad_src, grad_ud, grad_lr, win_bias, sum_bias, rows, table, tab, sum_acc, sum_low, ry, rz, ry_sum, ry_low, sg_src,
    ld_s, loc_s, side_ss, side_rs, sh_ss, sh_rs, in_ss, in_rs, halo_ss, halo_rs, gh_ss, gh_rs,
    za_ss, za_rs, ya_ss, ya_rs, ry_ss, ry_rs, rz_ss, rz_rs, oq_ss, oq_rs, ok_ss, ok_rs, sg_ss, sg_rs, out_s,
    from_up, from_down, from_next,
):
    row, col = lax.axis_index("row"), lax.axis_index("col")
    z, y = row // 2, col // 4
    me = lax.rem(row, 2) * 4 + lax.rem(col, 4)

    def ring(j):
        return (2 * z + j // 4, 4 * y + lax.rem(j, 4))

    def patch(dz, dy):
        return (row + 2 * dz, col + 4 * dy)

    def exists(dz, dy):
        ok = None
        for at, d, n in ((z, dz, 8), (y, dy, 4)):
            if d:
                here = (at > 0) if d < 0 else (at < n - 1)
                ok = here if ok is None else ok & here
        return ok

    def remote(src, dst, ss, rs, device):
        return pltpu.make_async_remote_copy(
            src_ref=src, dst_ref=dst, send_sem=ss, recv_sem=rs, device_id=device, device_id_type=MESH
        )

    barrier = pltpu.get_barrier_semaphore()

    def hello(device):
        pl.semaphore_signal(barrier, inc=1, device_id=device, device_id_type=MESH)

    each(1, 8, lambda o: hello(ring(lax.rem(me + o, 8))))
    each(1, 4, lambda o: hello((row, lax.rem(col + 4 * o, 16))))
    expected = jnp.int32(10)
    for dz in (-3, -2, 2, 3):
        there = (z + dz >= 0) & (z + dz <= 7)
        pl.when(there)(lambda dz=dz: hello(patch(dz, 0)))
        expected = expected + jnp.where(there, 1, 0)
    for dz, dy in NEAR:
        if dz:
            pl.when(exists(dz, dy))(lambda dz=dz, dy=dy: hello(patch(dz, dy)))
            expected = expected + jnp.where(exists(dz, dy), 1, 0)

    own_k = pltpu.make_async_copy(k, own.at[0], ld_s.at[0])
    own_v = pltpu.make_async_copy(v, own.at[1], ld_s.at[1])
    own_n = pltpu.make_async_copy(norm_in, own_norm.at[0], ld_s.at[2])
    own_o = pltpu.make_async_copy(offset_in, own_norm.at[1], ld_s.at[3])
    own_l = pltpu.make_async_copy(listed_in, own_listed, ld_s.at[4])
    for copy in (own_k, own_v, own_n, own_o, own_l):
        copy.start()

    def local_in(s, i):
        src = (k, v, q, go)[i].at[:, pl.ds(pl.multiple_of(me * 256 + s * 128, 128), 128)]
        return pltpu.make_async_copy(src, in_dst(s, i, me), loc_s.at[s, i])

    def in_dst(s, i, slot):
        if i < 2:
            return kv.at[s, i, slot]
        return qg_land.at[s, slot, :, pl.ds(128 * (i - 2), 128)]

    def d_in(s, i, o, slot):
        j = lax.rem(me + o, 8)
        src = (k, v, q, go)[i].at[:, pl.ds(pl.multiple_of(j * 256 + s * 128, 128), 128)]
        return remote(src, in_dst(s, i, slot), in_ss.at[s, i, o], in_rs.at[s, i, o], ring(j))

    for s in range(2):
        for i in range(4):
            local_in(s, i).start()

    def zero_acc(i):
        for s in range(2):
            for b in range(4):
                acc[s, b, pl.ds(pl.multiple_of(i * 128, 128), 128), :] = jnp.zeros((128, 128), F32)

    each(0, 5, zero_acc)

    for at, end, band, ud in ((z, 0, 0, 0), (z, 7, 3, 1)):

        @pl.when(at == end)
        def _(band=band, ud=ud):
            for b in range(6):
                side[band, b] = jnp.zeros((16, 128), F32)
            for s in range(2):
                qg[s, band] = jnp.zeros((640, 256), BF16)
                grad_ud[s, ud] = jnp.zeros((640, 128), BF16)

    for at, end, first, block, lr, ud in ((y, 0, 0, 0, 0, 512), (y, 3, 576, 5, 1, 576)):

        @pl.when(at == end)
        def _(first=first, block=block, lr=lr, ud=ud):
            for b in range(4):
                side[b, block] = jnp.zeros((16, 128), F32)
            for s in range(2):
                for b in range(4):
                    qg[s, b, first : first + 64] = jnp.zeros((64, 256), BF16)
                for a in range(2):
                    grad_lr[s, lr, a] = jnp.zeros((64, 128), BF16)
                    grad_ud[s, a, ud : ud + 64] = jnp.zeros((64, 128), BF16)

    query_at = lax.broadcasted_iota(jnp.int32, (256, 128), 0)
    key_at = lax.broadcasted_iota(jnp.int32, (256, 128), 1)
    dc = 8 * (query_at // 64 - 1) + query_at % 8 - key_at % 16
    for j in range(3):
        dr = 8 * (j - 1) + (query_at % 64) // 8 - key_at // 16
        near = (jnp.abs(dr) <= 8) & (jnp.abs(dc) <= 8)
        win_bias[j] = jnp.where(near, F32(0), F32(OFF))

    for copy in (own_k, own_v, own_n, own_o, own_l):
        copy.wait()
    norm = own_norm[0].T * LOG2E
    offset = own_norm[1].T
    for j in range(8):
        side_src[j] = jnp.zeros((16, 128), F32)
        side_src[j, 0:2] = norm[2 * j : 2 * j + 2]
        side_src[j, 2:4] = offset[2 * j : 2 * j + 2]
        side_src[j, 4:5, 0:64] = own_listed[...].astype(F32)
        for i in range(2):
            total = jnp.sum(own[i, :, 256 * j : 256 * j + 256].astype(F32), axis=0, keepdims=True)
            total = (total * POOL).astype(BF16).astype(F32)
            side_src[j, 8 + i : 9 + i] = total[:, :128]
            side_src[j, 10 + i : 11 + i] = total[:, 128:]

    pl.semaphore_wait(barrier, expected)

    def d_side(o, slot):
        j = lax.rem(me + o, 8)
        dst = side.at[1 + slot // 4, 1 + lax.rem(slot, 4)]
        return remote(side_src.at[j], dst, side_ss.at[o], side_rs.at[o], ring(j))

    each(1, 8, lambda o: d_side(o, me).start())

    def start_in(s, first):
        def body(o):
            d_in(s, first, o, me).start()
            d_in(s, first + 1, o, me).start()

        each(1, 8, body)

    def wait_in(s, first):
        def body(o):
            slot = lax.rem(me + 8 - o, 8)
            d_in(s, first, o, slot).wait_recv()
            d_in(s, first + 1, o, slot).wait_recv()

        each(1, 8, body)
        local_in(s, first).wait()
        local_in(s, first + 1).wait()


    def tell(when, steps, flag):
        @pl.when(when)
        def _():
            pl.semaphore_signal(flag, inc=1, device_id=patch(steps, 0), device_id_type=MESH)

    def told(when, flag):
        @pl.when(when)
        def _():
            pl.semaphore_wait(flag, 1)

    tell(z >= 3, -3, from_down)
    tell(z <= 4, 3, from_up)
    start_in(0, 2)
    told(z <= 4, from_down)
    told(z >= 3, from_up)
    tell(z == 1, -1, from_next)
    tell(z == 6, 1, from_next)
    told((z == 0) | (z == 7), from_next)

    side[1 + me // 4, 1 + lax.rem(me, 4)] = side_src[me]
    each(1, 8, lambda o: d_side(o, lax.rem(me + 8 - o, 8)).wait_recv())
    for t in range(8):
        for s in range(2):
            for i in range(2):
                one = side[1 + t // 4, 1 + t % 4, 8 + 2 * s + i : 9 + 2 * s + i]
                rows[8 * s + t : 8 * s + t + 1, 128 * i : 128 * i + 128] = one
    table[y, z] = rows[...].astype(BF16)

    def d_za(o, slot):
        device = (lax.rem(row + 2 * o, 16), col)
        return remote(table.at[y, z], table.at[y, slot], za_ss.at[o], za_rs.at[o], device)

    each(1, 8, lambda o: d_za(o, z).start())
    start_in(1, 2)
    start_in(0, 0)
    start_in(1, 0)

    def d_ya(o, n, slot):
        device = (row, lax.rem(col + 4 * o, 16))
        return remote(table.at[y, n], table.at[slot, n], ya_ss.at[o, n], ya_rs.at[o, n], device)

    def forward(n):
        for o in range(1, 4):
            d_ya(o, n, y).start()

    forward(z)

    def split(s):
        def body(t):
            block = qg_land[s, t].astype(F32).reshape(8, 16, 256)
            base = pl.multiple_of(64 + 128 * lax.rem(t, 4), 64)
            for h in range(2):
                half = block[:, 8 * h : 8 * h + 8].reshape(64, 256).astype(BF16)
                qg[s, 1 + t // 4, pl.ds(pl.multiple_of(base + 64 * h, 64), 64), :] = half

        each(0, 8, body)

    def d_halo(s, n):
        dz, dy = NEAR[n]
        band, to_band = {-1: 1, 1: 2}.get(dz), {-1: 3, 1: 0}.get(dz)
        at, to = {0: (64, 64), -1: (64, 576), 1: (512, 0)}[dy]
        size = 64 if dy else 512
        if dz:
            src, dst = qg.at[s, band, pl.ds(at, size)], qg.at[s, to_band, pl.ds(to, size)]
        else:
            src, dst = qg.at[s, pl.ds(1, 2), pl.ds(at, size)], qg.at[s, pl.ds(1, 2), pl.ds(to, size)]
        return remote(src, dst, halo_ss.at[s, n], halo_rs.at[s, n], patch(dz, dy))

    def d_sh(n):
        dz, dy = NEAR[n]
        band, to_band = {-1: 1, 1: 2}.get(dz), {-1: 3, 1: 0}.get(dz)
        at, to = {0: (1, 1), -1: (1, 5), 1: (4, 0)}[dy]
        size = 1 if dy else 4
        if dz:
            src, dst = side.at[band, pl.ds(at, size)], side.at[to_band, pl.ds(to, size)]
        else:
            src, dst = side.at[pl.ds(1, 2), pl.ds(at, size)], side.at[pl.ds(1, 2), pl.ds(to, size)]
        return remote(src, dst, sh_ss.at[n], sh_rs.at[n], patch(dz, dy))

    def start_near(make):
        for n, (dz, dy) in enumerate(NEAR):
            pl.when(exists(dz, dy))(lambda n=n: make(n).start())

    def wait_near(make):
        for n, (dz, dy) in enumerate(NEAR):
            pl.when(exists(-dz, -dy))(lambda n=n: make(n).wait_recv())

    def spread(band, block, halves):
        columns = side[band, block].T
        side_col[...] = columns
        for s in range(2):
            for i in range(2):
                wide = jnp.broadcast_to(columns[:, 2 * i + s : 2 * i + s + 1], (128, 128)).reshape(8, 16, 128)
                for h, at in halves:
                    lanes[s, i, band, pl.ds(at, 64), :] = wide[:, 8 * h : 8 * h + 8].reshape(64, 128)

    def spread_own(t):
        band, block = 1 + t // 4, 1 + lax.rem(t, 4)
        base = 128 * block - 64
        spread(band, block, ((0, pl.multiple_of(base, 64)), (1, pl.multiple_of(base + 64, 64))))
        at = lax.broadcasted_iota(jnp.int32, (64, 256), 1)
        number = (2 * ((at // 8) % 8) + (at % 8) // 4) * 16 + 4 * (at // 64) + at % 4
        hit = jnp.where(number.astype(F32) == side_col[0:64, 4:5], F32(0), F32(OFF))
        sum_bias[t] = jnp.broadcast_to(jnp.max(hit, axis=0, keepdims=True), (8, 256))

    def spread_halo():
        for band in (0, 3):

            def middle(n, band=band):
                base = 128 * n - 64
                spread(band, n, ((0, pl.multiple_of(base, 64)), (1, pl.multiple_of(base + 64, 64))))

            each(1, 5, middle, 4)

        def edges(band):
            spread(band, 0, ((1, 0),))
            spread(band, 5, ((0, 576),))

        each(0, 4, edges, 4)

    def d_grad(s, n):
        dz, dy = NEAR[n]
        band = {-1: 0, 1: 3}.get(dz)
        at, size = {0: (64, 512), -1: (0, 64), 1: (576, 64)}[dy]
        if dz:
            src = grad_src.at[s, band, pl.ds(at, size)]
            side_at = 1 if dz < 0 else 0
            to = {0: 0, -1: 576, 1: 512}[dy]
            dst = grad_ud.at[s, side_at, pl.ds(to, size)]
        else:
            src = grad_src.at[s, pl.ds(1, 2), pl.ds(at, size)]
            dst = grad_lr.at[s, 1 if dy < 0 else 0]
        return remote(src, dst, gh_ss.at[s, n], gh_rs.at[s, n], patch(dz, dy))

    def start_grad(s):
        for band in (0, 3):
            grad_src[s, band] = acc[s, band].astype(BF16)
        for band in (1, 2):
            for at in (0, 576):
                grad_src[s, band, at : at + 64] = acc[s, band, at : at + 64].astype(BF16)
        start_near(lambda n: d_grad(s, n))

    def compute(s):
        def body(t, carry):
            a, b = t // 4, lax.rem(t, 4)
            queries = pl.ds(pl.multiple_of(128 * b, 128), 256)
            operand = jnp.concatenate([qg[s, a + j, queries] for j in range(3)], axis=0)
            norm = jnp.concatenate([lanes[s, 0, a + j, queries] for j in range(3)], axis=0)
            offset = jnp.concatenate([lanes[s, 1, a + j, queries] for j in range(3)], axis=0)
            bias = jnp.concatenate([win_bias[j] for j in range(3)], axis=0)
            grad_k, grad_v, grad_q = pair_tile(operand, kv[s, 0, t], kv[s, 1, t], norm, offset, bias)
            for j in range(3):
                acc[s, a + j, queries] = acc[s, a + j, queries] + grad_q[256 * j : 256 * j + 256]
            gkv_low[s, t, :, 0:128] = grad_k.astype(BF16)
            gkv_low[s, t, :, 128:256] = grad_v.astype(BF16)
            return carry

        lax.fori_loop(0, 8, body, 0, unroll=4)

    def summary(s):
        keys, values = tab[s, :, 0:128], tab[s, :, 128:256]
        for a in range(2):
            operand = qg[s, 1 + a, 64:576]
            norm, offset = lanes[s, 0, 1 + a, 64:576], lanes[s, 1, 1 + a, 64:576]
            bias = jnp.concatenate(
                [jnp.broadcast_to(sum_bias[4 * a + b, 0:1], (128, 256)) for b in range(4)], axis=0
            )
            grad_k, grad_v, grad_q = pair_tile(
                operand,
                keys,
                values,
                jnp.concatenate([norm, norm], axis=1),
                jnp.concatenate([offset, offset], axis=1),
                bias,
            )
            acc[s, 1 + a, 64:576] = acc[s, 1 + a, 64:576] + grad_q
            sum_acc[s, :, 0:128] = grad_k if a == 0 else sum_acc[s, :, 0:128] + grad_k
            sum_acc[s, :, 128:256] = grad_v if a == 0 else sum_acc[s, :, 128:256] + grad_v

    def d_ry(s, o, slot):
        to = lax.rem(y + o, 4)
        src = sum_low.at[s, pl.ds(pl.multiple_of(64 * to, 64), 64)]
        return remote(src, ry.at[s, slot], ry_ss.at[s, o], ry_rs.at[s, o], (row, lax.rem(col + 4 * o, 16)))

    def d_rz(o, slot):
        to = lax.rem(z + o, 8)
        return remote(ry_low.at[to], rz.at[slot], rz_ss.at[o], rz_rs.at[o], (lax.rem(row + 2 * o, 16), col))

    def start_ry(s):
        sum_low[s] = sum_acc[s].astype(BF16)
        each(1, 4, lambda o: d_ry(s, o, y).start())

    def mid_reduce():
        totals = []
        for s in range(2):
            each(1, 4, lambda o: d_ry(s, o, lax.rem(y + 4 - o, 4)).wait_recv())
            total = sum_acc[s, pl.ds(pl.multiple_of(64 * y, 64), 64), :]
            ry[s, y] = jnp.zeros((64, 256), BF16)
            for n in range(4):
                total = total + ry[s, n].astype(F32)
            totals.append(total.reshape(8, 8, 256))
        total = jnp.concatenate(totals, axis=1)
        ry_sum[...] = total
        ry_low[...] = total.astype(BF16)
        each(1, 8, lambda o: d_rz(o, z).start())

    def end_reduce():
        rz[z] = jnp.zeros((16, 256), BF16)
        each(1, 8, lambda o: d_rz(o, lax.rem(z + 8 - o, 8)).wait_recv())
        total = ry_sum[z]
        for n in range(8):
            total = total + rz[n].astype(F32)
        total = total * POOL
        for s in range(2):
            for t in range(8):
                sg_src[t, s] = jnp.broadcast_to(total[8 * s + t : 8 * s + t + 1], (8, 256))

    def d_oq(s, o, slot):
        j = lax.rem(me + o, 8)
        return remote(gq_low.at[s, j], gq_out.at[2 * slot + s], oq_ss.at[s, o], oq_rs.at[s, o], ring(j))

    def l_oq(s):
        return pltpu.make_async_copy(gq_low.at[s, me], gq_out.at[2 * me + s], out_s.at[s])

    def d_ok(s, o, slot):
        j = lax.rem(me + o, 8)
        return remote(gkv_low.at[s, j], gkv_out.at[2 * slot + s], ok_ss.at[s, o], ok_rs.at[s, o], ring(j))

    def l_ok(s):
        return pltpu.make_async_copy(gkv_low.at[s, me], gkv_out.at[2 * me + s], out_s.at[2 + s])

    def d_sg(o, slot):
        j = lax.rem(me + o, 8)
        return remote(sg_src.at[j], sg_out.at[slot], sg_ss.at[o], sg_rs.at[o], ring(j))

    l_sg = pltpu.make_async_copy(sg_src.at[me], sg_out.at[me], out_s.at[4])

    def start_ok(s):
        each(1, 8, lambda o: d_ok(s, o, me).start())
        l_ok(s).start()

    def combine(s):
        def body(t):
            a, b = t // 4, lax.rem(t, 4)
            total = acc[s, 1 + a, pl.ds(pl.multiple_of(64 + 128 * b, 64), 128), :]
            total = total + grad_ud[s, a, pl.ds(pl.multiple_of(128 * b, 128), 128), :].astype(F32)
            left = grad_lr[s, 0, a].astype(F32) + grad_ud[s, a, 512:576].astype(F32)
            right = grad_lr[s, 1, a].astype(F32) + grad_ud[s, a, 576:640].astype(F32)
            none = jnp.zeros((64, 128), F32)
            left = jnp.where(b == 0, left, none)
            right = jnp.where(b == 3, right, none)
            gq_low[s, t] = (total + jnp.concatenate([left, right], axis=0)).astype(BF16)

        each(0, 8, body)
        each(1, 8, lambda o: d_oq(s, o, me).start())
        l_oq(s).start()

    start_near(d_sh)
    wait_in(0, 2)
    split(0)
    start_near(lambda n: d_halo(0, n))
    each(0, 8, spread_own, 4)
    wait_in(1, 2)
    split(1)
    start_near(lambda n: d_halo(1, n))
    wait_near(d_sh)
    spread_halo()

    def pass_on(o):
        source = lax.rem(z + 8 - o, 8)
        d_za(o, source).wait_recv()
        forward(source)

    each(1, 8, pass_on)
    wait_in(0, 0)
    wait_near(lambda n: d_halo(0, n))
    compute(0)
    start_ok(0)
    start_grad(0)
    for o in range(1, 4):
        each(0, 8, lambda n, o=o: d_ya(o, n, lax.rem(y + 4 - o, 4)).wait_recv())
    for s in range(2):
        for n in range(4):
            part = table[n].astype(F32)[:, 8 * s : 8 * s + 8]
            tab[s, 64 * n : 64 * n + 64] = part.reshape(64, 256).astype(BF16)
    for s in range(2):
        summary(s)
        start_ry(s)

    wait_in(1, 0)
    wait_near(lambda n: d_halo(1, n))
    compute(1)
    start_ok(1)
    start_grad(1)
    mid_reduce()
    wait_near(lambda n: d_grad(0, n))
    combine(0)
    wait_near(lambda n: d_grad(1, n))
    combine(1)
    end_reduce()
    each(1, 8, lambda o: d_sg(o, me).start())
    l_sg.start()

    def drain_ring(o):
        slot = lax.rem(me + 8 - o, 8)
        d_side(o, me).wait_send()
        d_za(o, z).wait_send()
        for s in range(2):
            for i in range(4):
                d_in(s, i, o, me).wait_send()
            d_oq(s, o, me).wait_send()
            d_oq(s, o, slot).wait_recv()
            d_ok(s, o, me).wait_send()
            d_ok(s, o, slot).wait_recv()
        d_rz(o, z).wait_send()
        d_sg(o, me).wait_send()
        d_sg(o, slot).wait_recv()

    each(1, 8, drain_ring)

    def drain_y(o):
        each(0, 8, lambda n: d_ya(o, n, y).wait_send())
        for s in range(2):
            d_ry(s, o, y).wait_send()

    each(1, 4, drain_y)
    for s in range(2):
        l_oq(s).wait()
        l_ok(s).wait()
        for n, (dz, dy) in enumerate(NEAR):

            def drain_near(n=n, s=s):
                d_halo(s, n).wait_send()
                d_grad(s, n).wait_send()
                if s == 0:
                    d_sh(n).wait_send()

            pl.when(exists(dz, dy))(drain_near)
    l_sg.wait()


def finish(gq, gkv, sg, out_q, out_k, out_v):
    heads = gkv.shape[0]
    for n in range(heads):
        total = gkv[n].astype(F32) + sg[n // 2, n % 2, 0:1]
        at = slice(128 * n, 128 * n + 128)
        out_k[:, :, at] = total[:, :128].reshape(8, 16, 128)
        out_v[:, :, at] = total[:, 128:].reshape(8, 16, 128)
        for h in range(2):
            out_q[:, 8 * h : 8 * h + 8, at] = gq[n, 64 * h : 64 * h + 64].astype(F32).reshape(8, 8, 128)


def on_device(query_rows, key_rows, value_rows, grad_out, log_norm, grad_offset, listed):
    flat = [x.reshape(128, 2048) for x in (query_rows, key_rows, value_rows, grad_out)]
    flat += [log_norm.reshape(128, 16), grad_offset.reshape(128, 16), listed]
    dma = pltpu.SemaphoreType.DMA
    gq, gkv, sg = pl.pallas_call(
        kernel,
        out_shape=(
            jax.ShapeDtypeStruct((16, 128, 128), BF16),
            jax.ShapeDtypeStruct((16, 128, 256), BF16),
            jax.ShapeDtypeStruct((8, 2, 8, 256), F32),
        ),
        in_specs=[pl.BlockSpec(memory_space=pltpu.HBM)] * 7,
        out_specs=(pl.BlockSpec(memory_space=pltpu.HBM),) * 3,
        scratch_shapes=[
            pltpu.VMEM((2, 128, 2048), BF16),
            pltpu.VMEM((2, 128, 16), F32),
            pltpu.VMEM((1, 64), jnp.int32),
            pltpu.VMEM((8, 16, 128), F32),
            pltpu.VMEM((4, 6, 16, 128), F32),
            pltpu.VMEM((128, 16), F32),
            pltpu.VMEM((2, 8, 128, 256), BF16),
            pltpu.VMEM((2, 4, 640, 256), BF16),
            pltpu.VMEM((2, 2, 8, 128, 128), BF16),
            pltpu.VMEM((2, 2, 4, 640, 128), F32),
            pltpu.VMEM((2, 4, 640, 128), F32),
            pltpu.VMEM((2, 8, 128, 128), BF16),
            pltpu.VMEM((2, 8, 128, 256), BF16),
            pltpu.VMEM((2, 4, 640, 128), BF16),
            pltpu.VMEM((2, 2, 640, 128), BF16),
            pltpu.VMEM((2, 2, 2, 64, 128), BF16),
            pltpu.VMEM((3, 256, 128), F32),
            pltpu.VMEM((8, 8, 256), F32),
            pltpu.VMEM((16, 256), F32),
            pltpu.VMEM((4, 8, 16, 256), BF16),
            pltpu.VMEM((2, 256, 256), BF16),
            pltpu.VMEM((2, 256, 256), F32),
            pltpu.VMEM((2, 256, 256), BF16),
            pltpu.VMEM((2, 4, 64, 256), BF16),
            pltpu.VMEM((8, 16, 256), BF16),
            pltpu.VMEM((8, 16, 256), F32),
            pltpu.VMEM((8, 16, 256), BF16),
            pltpu.VMEM((8, 2, 8, 256), F32),
            dma((5,)), dma((2, 4)), dma((8,)), dma((8,)), dma((8,)), dma((8,)), dma((2, 4, 8)), dma((2, 4, 8)),
            dma((2, 8)), dma((2, 8)), dma((2, 8)), dma((2, 8)),
            dma((8,)), dma((8,)), dma((4, 8)), dma((4, 8)), dma((2, 4)), dma((2, 4)), dma((8,)), dma((8,)),
            dma((2, 8)), dma((2, 8)), dma((2, 8)), dma((2, 8)), dma((8,)), dma((8,)), dma((5,)),
            pltpu.SemaphoreType.REGULAR, pltpu.SemaphoreType.REGULAR, pltpu.SemaphoreType.REGULAR,
        ],
        compiler_params=pltpu.CompilerParams(
            collective_id=0, has_side_effects=True, vmem_limit_bytes=60 * 2**20
        ),
        name="exchange",
    )(*flat)
    steps = 2
    heads = 16 // steps
    wide = heads * 128
    return pl.pallas_call(
        finish,
        grid=(steps,),
        out_shape=(jax.ShapeDtypeStruct((8, 16, 2048), F32),) * 3,
        in_specs=[
            pl.BlockSpec((heads, 128, 128), lambda i: (i, 0, 0)),
            pl.BlockSpec((heads, 128, 256), lambda i: (i, 0, 0)),
            pl.BlockSpec((heads // 2, 2, 8, 256), lambda i: (i, 0, 0, 0)),
        ],
        out_specs=(pl.BlockSpec((8, 16, wide), lambda i: (0, 0, i)),) * 3,
        compiler_params=pltpu.CompilerParams(vmem_limit_bytes=60 * 2**20),
        name="finish",
    )(gq, gkv, sg)


def solution(mesh):
    tokens = P("row", "col", None)
    return jax.shard_map(
        on_device,
        mesh=mesh,
        in_specs=(tokens,) * 6 + (P(("row", "col"), None),),
        out_specs=(tokens,) * 3,
        check_vma=False,
    )
```

```python
import math

import jax
import jax.numpy as jnp
from jax import lax
from jax.experimental import pallas as pl
from jax.experimental.pallas import tpu as pltpu
from jax.sharding import PartitionSpec as P

MESH = pl.DeviceIdType.MESH
F32 = jnp.float32
BF16 = jnp.bfloat16
LOG2E = math.log2(math.e)
SCALE = 1.0 / math.sqrt(128)
POOL = 1.0 / math.sqrt(128)
OFF = -1e30
NT = (((1,), (1,)), ((), ()))
TN = (((0,), (0,)), ((), ()))
NEAR = ((-1, 0), (1, 0), (0, -1), (0, 1), (-1, -1), (-1, 1), (1, -1), (1, 1))


def each(low, high, body, unroll=1):
    def step(i, carry):
        body(i)
        return carry

    lax.fori_loop(low, high, step, 0, unroll=unroll)


def pair_tile(qg, keys, values, norm, offset, bias):
    q, go = qg[:, :128], qg[:, 128:]
    scores = lax.dot_general(q, keys, NT, preferred_element_type=F32)
    grad_weights = lax.dot_general(go, values, NT, preferred_element_type=F32)
    weights = jnp.exp2(scores * (SCALE * LOG2E) - norm + bias)
    grads = (weights * (grad_weights - offset) * SCALE).astype(BF16)
    grad_q = jnp.dot(grads, keys, preferred_element_type=F32)
    grad_k = lax.dot_general(grads, q, TN, preferred_element_type=F32)
    grad_v = lax.dot_general(weights.astype(BF16), go, TN, preferred_element_type=F32)
    return grad_k, grad_v, grad_q


def kernel(
    q, k, v, go, norm_in, offset_in, listed_in,
    gq_out, gkv_out, sg_out,
    own, own_norm, own_listed, side_src, side, side_col, qg_land, qg, kv, lanes, acc, gq_low, gkv_low,
    grad_src, grad_ud, grad_lr, win_bias, sum_bias, rows, table, tab, sum_acc, sum_low, ry, rz, ry_sum, ry_low, sg_src,
    ld_s, loc_s, side_ss, side_rs, sh_ss, sh_rs, in_ss, in_rs, halo_ss, halo_rs, gh_ss, gh_rs,
    za_ss, za_rs, ya_ss, ya_rs, ry_ss, ry_rs, rz_ss, rz_rs, oq_ss, oq_rs, ok_ss, ok_rs, sg_ss, sg_rs, out_s,
    from_up, from_down, from_next,
):
    row, col = lax.axis_index("row"), lax.axis_index("col")
    z, y = row // 2, col // 4
    me = lax.rem(row, 2) * 4 + lax.rem(col, 4)

    def ring(j):
        return (2 * z + j // 4, 4 * y + lax.rem(j, 4))

    def patch(dz, dy):
        return (row + 2 * dz, col + 4 * dy)

    def exists(dz, dy):
        ok = None
        for at, d, n in ((z, dz, 8), (y, dy, 4)):
            if d:
                here = (at > 0) if d < 0 else (at < n - 1)
                ok = here if ok is None else ok & here
        return ok

    def remote(src, dst, ss, rs, device):
        return pltpu.make_async_remote_copy(
            src_ref=src, dst_ref=dst, send_sem=ss, recv_sem=rs, device_id=device, device_id_type=MESH
        )

    barrier = pltpu.get_barrier_semaphore()

    def hello(device):
        pl.semaphore_signal(barrier, inc=1, device_id=device, device_id_type=MESH)

    each(1, 8, lambda o: hello(ring(lax.rem(me + o, 8))))
    each(1, 4, lambda o: hello((row, lax.rem(col + 4 * o, 16))))
    expected = jnp.int32(10)
    for dz in (-3, -2, 2, 3):
        there = (z + dz >= 0) & (z + dz <= 7)
        pl.when(there)(lambda dz=dz: hello(patch(dz, 0)))
        expected = expected + jnp.where(there, 1, 0)
    for dz, dy in NEAR:
        if dz:
            pl.when(exists(dz, dy))(lambda dz=dz, dy=dy: hello(patch(dz, dy)))
            expected = expected + jnp.where(exists(dz, dy), 1, 0)

    own_k = pltpu.make_async_copy(k, own.at[0], ld_s.at[0])
    own_v = pltpu.make_async_copy(v, own.at[1], ld_s.at[1])
    own_n = pltpu.make_async_copy(norm_in, own_norm.at[0], ld_s.at[2])
    own_o = pltpu.make_async_copy(offset_in, own_norm.at[1], ld_s.at[3])
    own_l = pltpu.make_async_copy(listed_in, own_listed, ld_s.at[4])
    for copy in (own_k, own_v, own_n, own_o, own_l):
        copy.start()

    def local_in(s, i):
        src = (k, v, q, go)[i].at[:, pl.ds(pl.multiple_of(me * 256 + s * 128, 128), 128)]
        return pltpu.make_async_copy(src, in_dst(s, i, me), loc_s.at[s, i])

    def in_dst(s, i, slot):
        if i < 2:
            return kv.at[s, i, slot]
        return qg_land.at[s, slot, :, pl.ds(128 * (i - 2), 128)]

    def d_in(s, i, o, slot):
        j = lax.rem(me + o, 8)
        src = (k, v, q, go)[i].at[:, pl.ds(pl.multiple_of(j * 256 + s * 128, 128), 128)]
        return remote(src, in_dst(s, i, slot), in_ss.at[s, i, o], in_rs.at[s, i, o], ring(j))

    for s in range(2):
        for i in range(4):
            local_in(s, i).start()

    def zero_acc(i):
        for s in range(2):
            for b in range(4):
                acc[s, b, pl.ds(pl.multiple_of(i * 128, 128), 128), :] = jnp.zeros((128, 128), F32)

    each(0, 5, zero_acc)

    for at, end, band, ud in ((z, 0, 0, 0), (z, 7, 3, 1)):

        @pl.when(at == end)
        def _(band=band, ud=ud):
            for b in range(6):
                side[band, b] = jnp.zeros((16, 128), F32)
            for s in range(2):
                qg[s, band] = jnp.zeros((640, 256), BF16)
                grad_ud[s, ud] = jnp.zeros((640, 128), BF16)

    for at, end, first, block, lr, ud in ((y, 0, 0, 0, 0, 512), (y, 3, 576, 5, 1, 576)):

        @pl.when(at == end)
        def _(first=first, block=block, lr=lr, ud=ud):
            for b in range(4):
                side[b, block] = jnp.zeros((16, 128), F32)
            for s in range(2):
                for b in range(4):
                    qg[s, b, first : first + 64] = jnp.zeros((64, 256), BF16)
                for a in range(2):
                    grad_lr[s, lr, a] = jnp.zeros((64, 128), BF16)
                    grad_ud[s, a, ud : ud + 64] = jnp.zeros((64, 128), BF16)

    query_at = lax.broadcasted_iota(jnp.int32, (256, 128), 0)
    key_at = lax.broadcasted_iota(jnp.int32, (256, 128), 1)
    dc = 8 * (query_at // 64 - 1) + query_at % 8 - key_at % 16
    for j in range(3):
        dr = 8 * (j - 1) + (query_at % 64) // 8 - key_at // 16
        near = (jnp.abs(dr) <= 8) & (jnp.abs(dc) <= 8)
        win_bias[j] = jnp.where(near, F32(0), F32(OFF))

    for copy in (own_k, own_v, own_n, own_o, own_l):
        copy.wait()
    norm = own_norm[0].T * LOG2E
    offset = own_norm[1].T
    for j in range(8):
        side_src[j] = jnp.zeros((16, 128), F32)
        side_src[j, 0:2] = norm[2 * j : 2 * j + 2]
        side_src[j, 2:4] = offset[2 * j : 2 * j + 2]
        side_src[j, 4:5, 0:64] = own_listed[...].astype(F32)
        for i in range(2):
            total = jnp.sum(own[i, :, 256 * j : 256 * j + 256].astype(F32), axis=0, keepdims=True)
            total = (total * POOL).astype(BF16).astype(F32)
            side_src[j, 8 + i : 9 + i] = total[:, :128]
            side_src[j, 10 + i : 11 + i] = total[:, 128:]

    pl.semaphore_wait(barrier, expected)

    def d_side(o, slot):
        j = lax.rem(me + o, 8)
        dst = side.at[1 + slot // 4, 1 + lax.rem(slot, 4)]
        return remote(side_src.at[j], dst, side_ss.at[o], side_rs.at[o], ring(j))

    each(1, 8, lambda o: d_side(o, me).start())

    def start_in(s, first):
        def body(o):
            d_in(s, first, o, me).start()
            d_in(s, first + 1, o, me).start()

        each(1, 8, body)

    def wait_in(s, first):
        def body(o):
            slot = lax.rem(me + 8 - o, 8)
            d_in(s, first, o, slot).wait_recv()
            d_in(s, first + 1, o, slot).wait_recv()

        each(1, 8, body)
        local_in(s, first).wait()
        local_in(s, first + 1).wait()


    def tell(when, steps, flag):
        @pl.when(when)
        def _():
            pl.semaphore_signal(flag, inc=1, device_id=patch(steps, 0), device_id_type=MESH)

    def told(when, flag):
        @pl.when(when)
        def _():
            pl.semaphore_wait(flag, 1)

    tell(z >= 3, -3, from_down)
    tell(z <= 4, 3, from_up)
    start_in(0, 2)
    told(z <= 4, from_down)
    told(z >= 3, from_up)
    tell(z == 1, -1, from_next)
    tell(z == 6, 1, from_next)
    told((z == 0) | (z == 7), from_next)

    side[1 + me // 4, 1 + lax.rem(me, 4)] = side_src[me]
    each(1, 8, lambda o: d_side(o, lax.rem(me + 8 - o, 8)).wait_recv())
    for t in range(8):
        for s in range(2):
            for i in range(2):
                one = side[1 + t // 4, 1 + t % 4, 8 + 2 * s + i : 9 + 2 * s + i]
                rows[8 * s + t : 8 * s + t + 1, 128 * i : 128 * i + 128] = one
    table[y, z] = rows[...].astype(BF16)

    def d_za(o, slot):
        device = (lax.rem(row + 2 * o, 16), col)
        return remote(table.at[y, z], table.at[y, slot], za_ss.at[o], za_rs.at[o], device)

    each(1, 8, lambda o: d_za(o, z).start())
    start_in(1, 2)
    start_in(0, 0)
    start_in(1, 0)

    def d_ya(o, n, slot):
        device = (row, lax.rem(col + 4 * o, 16))
        return remote(table.at[y, n], table.at[slot, n], ya_ss.at[o, n], ya_rs.at[o, n], device)

    def forward(n):
        for o in range(1, 4):
            d_ya(o, n, y).start()

    forward(z)

    def split(s):
        def body(t):
            block = qg_land[s, t].astype(F32).reshape(8, 16, 256)
            base = pl.multiple_of(64 + 128 * lax.rem(t, 4), 64)
            for h in range(2):
                half = block[:, 8 * h : 8 * h + 8].reshape(64, 256).astype(BF16)
                qg[s, 1 + t // 4, pl.ds(pl.multiple_of(base + 64 * h, 64), 64), :] = half

        each(0, 8, body)

    def d_halo(s, n):
        dz, dy = NEAR[n]
        band, to_band = {-1: 1, 1: 2}.get(dz), {-1: 3, 1: 0}.get(dz)
        at, to = {0: (64, 64), -1: (64, 576), 1: (512, 0)}[dy]
        size = 64 if dy else 512
        if dz:
            src, dst = qg.at[s, band, pl.ds(at, size)], qg.at[s, to_band, pl.ds(to, size)]
        else:
            src, dst = qg.at[s, pl.ds(1, 2), pl.ds(at, size)], qg.at[s, pl.ds(1, 2), pl.ds(to, size)]
        return remote(src, dst, halo_ss.at[s, n], halo_rs.at[s, n], patch(dz, dy))

    def d_sh(n):
        dz, dy = NEAR[n]
        band, to_band = {-1: 1, 1: 2}.get(dz), {-1: 3, 1: 0}.get(dz)
        at, to = {0: (1, 1), -1: (1, 5), 1: (4, 0)}[dy]
        size = 1 if dy else 4
        if dz:
            src, dst = side.at[band, pl.ds(at, size)], side.at[to_band, pl.ds(to, size)]
        else:
            src, dst = side.at[pl.ds(1, 2), pl.ds(at, size)], side.at[pl.ds(1, 2), pl.ds(to, size)]
        return remote(src, dst, sh_ss.at[n], sh_rs.at[n], patch(dz, dy))

    def start_near(make):
        for n, (dz, dy) in enumerate(NEAR):
            pl.when(exists(dz, dy))(lambda n=n: make(n).start())

    def wait_near(make):
        for n, (dz, dy) in enumerate(NEAR):
            pl.when(exists(-dz, -dy))(lambda n=n: make(n).wait_recv())

    def spread(band, block, halves):
        columns = side[band, block].T
        side_col[...] = columns
        for s in range(2):
            for i in range(2):
                wide = jnp.broadcast_to(columns[:, 2 * i + s : 2 * i + s + 1], (128, 128)).reshape(8, 16, 128)
                for h, at in halves:
                    lanes[s, i, band, pl.ds(at, 64), :] = wide[:, 8 * h : 8 * h + 8].reshape(64, 128)

    def spread_own(t):
        band, block = 1 + t // 4, 1 + lax.rem(t, 4)
        base = 128 * block - 64
        spread(band, block, ((0, pl.multiple_of(base, 64)), (1, pl.multiple_of(base + 64, 64))))
        at = lax.broadcasted_iota(jnp.int32, (64, 256), 1)
        number = (2 * ((at // 8) % 8) + (at % 8) // 4) * 16 + 4 * (at // 64) + at % 4
        hit = jnp.where(number.astype(F32) == side_col[0:64, 4:5], F32(0), F32(OFF))
        sum_bias[t] = jnp.broadcast_to(jnp.max(hit, axis=0, keepdims=True), (8, 256))

    def spread_halo():
        for band in (0, 3):

            def middle(n, band=band):
                base = 128 * n - 64
                spread(band, n, ((0, pl.multiple_of(base, 64)), (1, pl.multiple_of(base + 64, 64))))

            each(1, 5, middle, 4)

        def edges(band):
            spread(band, 0, ((1, 0),))
            spread(band, 5, ((0, 576),))

        each(0, 4, edges, 4)

    def d_grad(s, n):
        dz, dy = NEAR[n]
        band = {-1: 0, 1: 3}.get(dz)
        at, size = {0: (64, 512), -1: (0, 64), 1: (576, 64)}[dy]
        if dz:
            src = grad_src.at[s, band, pl.ds(at, size)]
            side_at = 1 if dz < 0 else 0
            to = {0: 0, -1: 576, 1: 512}[dy]
            dst = grad_ud.at[s, side_at, pl.ds(to, size)]
        else:
            src = grad_src.at[s, pl.ds(1, 2), pl.ds(at, size)]
            dst = grad_lr.at[s, 1 if dy < 0 else 0]
        return remote(src, dst, gh_ss.at[s, n], gh_rs.at[s, n], patch(dz, dy))

    def start_grad(s):
        for band in (0, 3):
            grad_src[s, band] = acc[s, band].astype(BF16)
        for band in (1, 2):
            for at in (0, 576):
                grad_src[s, band, at : at + 64] = acc[s, band, at : at + 64].astype(BF16)
        start_near(lambda n: d_grad(s, n))

    def compute(s):
        def body(t, carry):
            a, b = t // 4, lax.rem(t, 4)
            queries = pl.ds(pl.multiple_of(128 * b, 128), 256)
            operand = jnp.concatenate([qg[s, a + j, queries] for j in range(3)], axis=0)
            norm = jnp.concatenate([lanes[s, 0, a + j, queries] for j in range(3)], axis=0)
            offset = jnp.concatenate([lanes[s, 1, a + j, queries] for j in range(3)], axis=0)
            bias = jnp.concatenate([win_bias[j] for j in range(3)], axis=0)
            grad_k, grad_v, grad_q = pair_tile(operand, kv[s, 0, t], kv[s, 1, t], norm, offset, bias)
            for j in range(3):
                acc[s, a + j, queries] = acc[s, a + j, queries] + grad_q[256 * j : 256 * j + 256]
            gkv_low[s, t, :, 0:128] = grad_k.astype(BF16)
            gkv_low[s, t, :, 128:256] = grad_v.astype(BF16)
            return carry

        lax.fori_loop(0, 8, body, 0, unroll=8)

    def summary(s):
        keys, values = tab[s, :, 0:128], tab[s, :, 128:256]
        for a in range(2):
            operand = qg[s, 1 + a, 64:576]
            norm, offset = lanes[s, 0, 1 + a, 64:576], lanes[s, 1, 1 + a, 64:576]
            bias = jnp.concatenate(
                [jnp.broadcast_to(sum_bias[4 * a + b, 0:1], (128, 256)) for b in range(4)], axis=0
            )
            grad_k, grad_v, grad_q = pair_tile(
                operand,
                keys,
                values,
                jnp.concatenate([norm, norm], axis=1),
                jnp.concatenate([offset, offset], axis=1),
                bias,
            )
            acc[s, 1 + a, 64:576] = acc[s, 1 + a, 64:576] + grad_q
            sum_acc[s, :, 0:128] = grad_k if a == 0 else sum_acc[s, :, 0:128] + grad_k
            sum_acc[s, :, 128:256] = grad_v if a == 0 else sum_acc[s, :, 128:256] + grad_v

    def d_ry(s, o, slot):
        to = lax.rem(y + o, 4)
        src = sum_low.at[s, pl.ds(pl.multiple_of(64 * to, 64), 64)]
        return remote(src, ry.at[s, slot], ry_ss.at[s, o], ry_rs.at[s, o], (row, lax.rem(col + 4 * o, 16)))

    def d_rz(o, slot):
        to = lax.rem(z + o, 8)
        return remote(ry_low.at[to], rz.at[slot], rz_ss.at[o], rz_rs.at[o], (lax.rem(row + 2 * o, 16), col))

    def start_ry(s):
        sum_low[s] = sum_acc[s].astype(BF16)
        each(1, 4, lambda o: d_ry(s, o, y).start())

    def mid_reduce():
        totals = []
        for s in range(2):
            each(1, 4, lambda o: d_ry(s, o, lax.rem(y + 4 - o, 4)).wait_recv())
            total = sum_acc[s, pl.ds(pl.multiple_of(64 * y, 64), 64), :]
            ry[s, y] = jnp.zeros((64, 256), BF16)
            for n in range(4):
                total = total + ry[s, n].astype(F32)
            totals.append(total.reshape(8, 8, 256))
        total = jnp.concatenate(totals, axis=1)
        ry_sum[...] = total
        ry_low[...] = total.astype(BF16)
        each(1, 8, lambda o: d_rz(o, z).start())

    def end_reduce():
        rz[z] = jnp.zeros((16, 256), BF16)
        each(1, 8, lambda o: d_rz(o, lax.rem(z + 8 - o, 8)).wait_recv())
        total = ry_sum[z]
        for n in range(8):
            total = total + rz[n].astype(F32)
        total = total * POOL
        for s in range(2):
            for t in range(8):
                sg_src[t, s] = jnp.broadcast_to(total[8 * s + t : 8 * s + t + 1], (8, 256))

    def d_oq(s, o, slot):
        j = lax.rem(me + o, 8)
        return remote(gq_low.at[s, j], gq_out.at[2 * slot + s], oq_ss.at[s, o], oq_rs.at[s, o], ring(j))

    def l_oq(s):
        return pltpu.make_async_copy(gq_low.at[s, me], gq_out.at[2 * me + s], out_s.at[s])

    def d_ok(s, o, slot):
        j = lax.rem(me + o, 8)
        return remote(gkv_low.at[s, j], gkv_out.at[2 * slot + s], ok_ss.at[s, o], ok_rs.at[s, o], ring(j))

    def l_ok(s):
        return pltpu.make_async_copy(gkv_low.at[s, me], gkv_out.at[2 * me + s], out_s.at[2 + s])

    def d_sg(o, slot):
        j = lax.rem(me + o, 8)
        return remote(sg_src.at[j], sg_out.at[slot], sg_ss.at[o], sg_rs.at[o], ring(j))

    l_sg = pltpu.make_async_copy(sg_src.at[me], sg_out.at[me], out_s.at[4])

    def start_ok(s):
        each(1, 8, lambda o: d_ok(s, o, me).start())
        l_ok(s).start()

    def combine(s):
        def body(t):
            a, b = t // 4, lax.rem(t, 4)
            total = acc[s, 1 + a, pl.ds(pl.multiple_of(64 + 128 * b, 64), 128), :]
            total = total + grad_ud[s, a, pl.ds(pl.multiple_of(128 * b, 128), 128), :].astype(F32)
            left = grad_lr[s, 0, a].astype(F32) + grad_ud[s, a, 512:576].astype(F32)
            right = grad_lr[s, 1, a].astype(F32) + grad_ud[s, a, 576:640].astype(F32)
            none = jnp.zeros((64, 128), F32)
            left = jnp.where(b == 0, left, none)
            right = jnp.where(b == 3, right, none)
            gq_low[s, t] = (total + jnp.concatenate([left, right], axis=0)).astype(BF16)

        each(0, 8, body)
        each(1, 8, lambda o: d_oq(s, o, me).start())
        l_oq(s).start()

    start_near(d_sh)
    wait_in(0, 2)
    split(0)
    start_near(lambda n: d_halo(0, n))
    each(0, 8, spread_own, 4)

    def pass_on(o):
        source = lax.rem(z + 8 - o, 8)
        d_za(o, source).wait_recv()
        forward(source)

    each(1, 8, pass_on)
    wait_in(1, 2)
    split(1)
    start_near(lambda n: d_halo(1, n))
    wait_near(d_sh)
    spread_halo()
    wait_in(0, 0)
    wait_near(lambda n: d_halo(0, n))
    compute(0)
    start_ok(0)
    start_grad(0)
    for o in range(1, 4):
        each(0, 8, lambda n, o=o: d_ya(o, n, lax.rem(y + 4 - o, 4)).wait_recv())
    for s in range(2):
        for n in range(4):
            part = table[n].astype(F32)[:, 8 * s : 8 * s + 8]
            tab[s, 64 * n : 64 * n + 64] = part.reshape(64, 256).astype(BF16)
    for s in range(2):
        summary(s)
        start_ry(s)

    wait_in(1, 0)
    wait_near(lambda n: d_halo(1, n))
    compute(1)
    start_ok(1)
    start_grad(1)
    mid_reduce()
    wait_near(lambda n: d_grad(0, n))
    combine(0)
    wait_near(lambda n: d_grad(1, n))
    combine(1)
    end_reduce()
    each(1, 8, lambda o: d_sg(o, me).start())
    l_sg.start()

    def drain_ring(o):
        slot = lax.rem(me + 8 - o, 8)
        d_side(o, me).wait_send()
        d_za(o, z).wait_send()
        for s in range(2):
            for i in range(4):
                d_in(s, i, o, me).wait_send()
            d_oq(s, o, me).wait_send()
            d_oq(s, o, slot).wait_recv()
            d_ok(s, o, me).wait_send()
            d_ok(s, o, slot).wait_recv()
        d_rz(o, z).wait_send()
        d_sg(o, me).wait_send()
        d_sg(o, slot).wait_recv()

    each(1, 8, drain_ring)

    def drain_y(o):
        each(0, 8, lambda n: d_ya(o, n, y).wait_send())
        for s in range(2):
            d_ry(s, o, y).wait_send()

    each(1, 4, drain_y)
    for s in range(2):
        l_oq(s).wait()
        l_ok(s).wait()
        for n, (dz, dy) in enumerate(NEAR):

            def drain_near(n=n, s=s):
                d_halo(s, n).wait_send()
                d_grad(s, n).wait_send()
                if s == 0:
                    d_sh(n).wait_send()

            pl.when(exists(dz, dy))(drain_near)
    l_sg.wait()


def finish(gq, gkv, sg, out_q, out_k, out_v):
    heads = gkv.shape[0]
    for n in range(heads):
        total = gkv[n].astype(F32) + sg[n // 2, n % 2, 0:1]
        at = slice(128 * n, 128 * n + 128)
        out_k[:, :, at] = total[:, :128].reshape(8, 16, 128)
        out_v[:, :, at] = total[:, 128:].reshape(8, 16, 128)
        for h in range(2):
            out_q[:, 8 * h : 8 * h + 8, at] = gq[n, 64 * h : 64 * h + 64].astype(F32).reshape(8, 8, 128)


def on_device(query_rows, key_rows, value_rows, grad_out, log_norm, grad_offset, listed):
    flat = [x.reshape(128, 2048) for x in (query_rows, key_rows, value_rows, grad_out)]
    flat += [log_norm.reshape(128, 16), grad_offset.reshape(128, 16), listed]
    dma = pltpu.SemaphoreType.DMA
    gq, gkv, sg = pl.pallas_call(
        kernel,
        out_shape=(
            jax.ShapeDtypeStruct((16, 128, 128), BF16),
            jax.ShapeDtypeStruct((16, 128, 256), BF16),
            jax.ShapeDtypeStruct((8, 2, 8, 256), F32),
        ),
        in_specs=[pl.BlockSpec(memory_space=pltpu.HBM)] * 7,
        out_specs=(pl.BlockSpec(memory_space=pltpu.HBM),) * 3,
        scratch_shapes=[
            pltpu.VMEM((2, 128, 2048), BF16),
            pltpu.VMEM((2, 128, 16), F32),
            pltpu.VMEM((1, 64), jnp.int32),
            pltpu.VMEM((8, 16, 128), F32),
            pltpu.VMEM((4, 6, 16, 128), F32),
            pltpu.VMEM((128, 16), F32),
            pltpu.VMEM((2, 8, 128, 256), BF16),
            pltpu.VMEM((2, 4, 640, 256), BF16),
            pltpu.VMEM((2, 2, 8, 128, 128), BF16),
            pltpu.VMEM((2, 2, 4, 640, 128), F32),
            pltpu.VMEM((2, 4, 640, 128), F32),
            pltpu.VMEM((2, 8, 128, 128), BF16),
            pltpu.VMEM((2, 8, 128, 256), BF16),
            pltpu.VMEM((2, 4, 640, 128), BF16),
            pltpu.VMEM((2, 2, 640, 128), BF16),
            pltpu.VMEM((2, 2, 2, 64, 128), BF16),
            pltpu.VMEM((3, 256, 128), F32),
            pltpu.VMEM((8, 8, 256), F32),
            pltpu.VMEM((16, 256), F32),
            pltpu.VMEM((4, 8, 16, 256), BF16),
            pltpu.VMEM((2, 256, 256), BF16),
            pltpu.VMEM((2, 256, 256), F32),
            pltpu.VMEM((2, 256, 256), BF16),
            pltpu.VMEM((2, 4, 64, 256), BF16),
            pltpu.VMEM((8, 16, 256), BF16),
            pltpu.VMEM((8, 16, 256), F32),
            pltpu.VMEM((8, 16, 256), BF16),
            pltpu.VMEM((8, 2, 8, 256), F32),
            dma((5,)), dma((2, 4)), dma((8,)), dma((8,)), dma((8,)), dma((8,)), dma((2, 4, 8)), dma((2, 4, 8)),
            dma((2, 8)), dma((2, 8)), dma((2, 8)), dma((2, 8)),
            dma((8,)), dma((8,)), dma((4, 8)), dma((4, 8)), dma((2, 4)), dma((2, 4)), dma((8,)), dma((8,)),
            dma((2, 8)), dma((2, 8)), dma((2, 8)), dma((2, 8)), dma((8,)), dma((8,)), dma((5,)),
            pltpu.SemaphoreType.REGULAR, pltpu.SemaphoreType.REGULAR, pltpu.SemaphoreType.REGULAR,
        ],
        compiler_params=pltpu.CompilerParams(
            collective_id=0, has_side_effects=True, vmem_limit_bytes=60 * 2**20
        ),
        name="exchange",
    )(*flat)
    steps = 2
    heads = 16 // steps
    wide = heads * 128
    return pl.pallas_call(
        finish,
        grid=(steps,),
        out_shape=(jax.ShapeDtypeStruct((8, 16, 2048), F32),) * 3,
        in_specs=[
            pl.BlockSpec((heads, 128, 128), lambda i: (i, 0, 0)),
            pl.BlockSpec((heads, 128, 256), lambda i: (i, 0, 0)),
            pl.BlockSpec((heads // 2, 2, 8, 256), lambda i: (i, 0, 0, 0)),
        ],
        out_specs=(pl.BlockSpec((8, 16, wide), lambda i: (0, 0, i)),) * 3,
        compiler_params=pltpu.CompilerParams(vmem_limit_bytes=60 * 2**20),
        name="finish",
    )(gq, gkv, sg)


def solution(mesh):
    tokens = P("row", "col", None)
    return jax.shard_map(
        on_device,
        mesh=mesh,
        in_specs=(tokens,) * 6 + (P(("row", "col"), None),),
        out_specs=(tokens,) * 3,
        check_vma=False,
    )
```
